32 devices in a mesh: dp: 2 (over x), expert: 16 (over z, y, core).
Axes of the slice: x: 2, y: 2, z: 4, core: 2. Of those that a mesh axis runs over, the one named last changes fastest.
Arguments:
- tokens: bfloat16 [4096, 1024], P(('dp', 'expert')), may hold values from -6 to 6
- grad_out: bfloat16 [4096, 1024], P(('dp', 'expert')), may hold values from -6 to 6
- expert_ids: int32 [4096, 8], P(('dp', 'expert')), may hold values from 0 to 15, all different within a row; in each aligned block of 128 rows (0 to 127, 128 to 255, ...) at most 72 rows name the same one
- gate_numer: int32 [4096, 8], P(('dp', 'expert')), may hold values from 1 to 16
- w_gate: bfloat16 [16, 1024, 384], P('expert', 'dp'), may hold values from -0.1875 to 0.1875
- w_up: bfloat16 [16, 1024, 384], P('expert', 'dp'), may hold values from -0.1875 to 0.1875
- w_down: bfloat16 [16, 1024, 384], P('expert', 'dp'), may hold values from -0.3125 to 0.3125
Outputs:
- grad_tokens: bfloat16 [4096, 1024], P(('dp', 'expert'))
- grad_gate: bfloat16 [16, 1024, 384], P('expert', 'dp')
- grad_up: bfloat16 [16, 1024, 384], P('expert', 'dp')
- grad_down: bfloat16 [16, 1024, 384], P('expert', 'dp')
The draws below stay inside these ranges and needn't reach their ends.
Inputs may be any that keep to these rules, and one draw needn't show every extreme that they name: `expert_ids`: each row names 8 different experts. Within the rows of one device no expert is named more than 72 times, and in every draw some expert is named exactly 72 times within some device's rows.
All inputs are finite; a program needn't handle non-finite values.
Results may differ from the reference program's by a relative error of at most 0.0065.
Values may be sent and summed in bfloat16 or wider, within the bound.
A program may use at most 128 MiB of HBM per device.

```python
import math
import jax
import jax.numpy as jnp
import numpy as np
from jax import lax

D = 1024
FF = 384
TOP = 8
TOK_DEV = 128
EXPERTS = 16
GROUP_TOKENS = 2048
TOKENS = 4096
CAP = 72
SLOTS = 1152
N_DP = 2


def plant(result, rng, low, top_value):
    longest = result.shape.index(max(result.shape))
    spots = []
    for shift in (0, 1):
        where = [jax.random.randint(jax.random.fold_in(rng, axis), (), 0, length) for axis, length in enumerate(result.shape)]
        where[longest] = (where[longest] + shift) % result.shape[longest]
        spots.append(tuple(where))
    return result.at[spots[0]].set(low).at[spots[1]].set(top_value)


def levels(key, extent, shards, least, largest):
    def one(dim, parts):
        draws = jax.random.uniform(jax.random.fold_in(jax.random.fold_in(key, 6), dim), (parts,), jnp.float32, least / len(shards), largest / len(shards))
        return jnp.repeat(jnp.exp(draws), extent[dim] // parts).reshape((-1,) + (1,) * (len(extent) - dim - 1))

    gain = one(*shards[0])
    for cut in shards[1:]:
        gain = gain * one(*cut)
    return gain


def routed_block(stream_key, own, number, rows, amount, top, reach, lean):
    order = jax.random.permutation(stream_key, amount)
    packed, usual = load_shares(amount, rows * top, reach, lean, True), load_shares(amount, rows * top, reach, lean, False)
    places = jnp.arange(amount)

    def named(lengths, rotation):
        used = int((lengths > 0).sum())
        fixed = max(1, used // 4)
        moved = fixed + (places - fixed + rotation * (used - fixed)) % max(1, amount - fixed)
        return jnp.zeros((amount,), jnp.int32).at[order[jnp.where(places < fixed, places, moved)]].set(jnp.asarray(lengths, jnp.int32))

    lengths = jnp.where(number % 4 == 0, named(packed, number // 4), named(usual, number - number // 4 - 1))
    mixed = jax.random.permutation(jax.random.fold_in(own, 3), amount)
    source_of, receiver = mixed[0:amount // 2 * 2:2], mixed[1:amount // 2 * 2:2]
    margin = jnp.minimum(lengths[source_of] - 1, reach - lengths[receiver]) // 2
    margin = jnp.where((source_of == order[0]) | (receiver == order[0]) | (lengths[receiver] == 0), 0, jnp.maximum(margin, 0))
    moved = jax.random.randint(jax.random.fold_in(own, 4), (amount // 2,), 0, 1 << 20) % (margin + 1)
    lengths = lengths.at[source_of].add(-moved).at[receiver].add(moved)
    items = jnp.searchsorted(jnp.cumsum(lengths), jnp.arange(rows * top), side="right").astype(jnp.int32)
    listing = items.reshape(top, rows).T
    listing = listing[jax.random.permutation(jax.random.fold_in(own, 1), rows)]
    rotation = jax.random.randint(jax.random.fold_in(own, 2), (rows, 1), 0, top)
    return jnp.take_along_axis(listing, (jnp.arange(top)[None, :] + rotation) % top, axis=1)


def load_shares(amount, total, most, slope, full):
    portions = [(1 << 20) // math.isqrt(standing ** slope) + 1 for standing in range(1, amount + 1)]
    largest = most if full else min(most, max(-(-total // amount), total * portions[0] // sum(portions)))
    least = 1 if total - largest >= amount - 1 else 0
    given, surplus = [largest] + [least] * (amount - 1), total - largest - least * (amount - 1)
    while surplus > 0:
        free = [i for i in range(1, amount) if given[i] < largest] or [i for i in range(1, amount) if given[i] < most]
        mass, left = sum([portions[i] for i in free]), surplus
        for i in free:
            extra = min(most - given[i], max(1, left * portions[i] // mass), surplus)
            given[i] = given[i] + extra
            surplus = surplus - extra
    return np.array(given)


def gaussian(stream_key, shape, scale, reach, cuts=(), kind=jnp.bfloat16):
    values = jax.random.normal(stream_key, shape, jnp.float32) * scale
    if len(cuts) > 0:
        values = levels(stream_key, shape, cuts, -0.22, 0.18) * values
    return jnp.clip(values, min=-reach, max=reach).astype(kind)


def setup_inputs(seed: int = 0) -> dict:
    splits = jax.random.split(jax.random.key(seed), 8)
    tokens = gaussian(splits[0], (TOKENS, D), 1.0, 6.0, ((0, 32),))
    grad_out = gaussian(splits[1], (TOKENS, D), 1.0, 6.0, ((0, 32),))
    expert_ids_keys = jax.random.split(jax.random.fold_in(splits[2], 1), TOKENS // TOK_DEV)
    expert_ids_turns = jax.random.permutation(jax.random.fold_in(splits[2], 3), TOKENS // TOK_DEV)
    expert_ids = jax.vmap(lambda own, number: routed_block(jax.random.fold_in(splits[2], 2), own, number, TOK_DEV, EXPERTS, TOP, CAP, 2))(expert_ids_keys, expert_ids_turns).reshape((TOKENS, TOP))
    gate_numer = plant(jax.random.randint(splits[3], (TOKENS, TOP), 1, 17), jax.random.fold_in(splits[3], 1), 1, 16).astype(jnp.int32)
    w_gate = gaussian(splits[4], (EXPERTS, D, FF), D ** -0.5, 0.1875, ((0, 16), (1, 2)))
    w_up = gaussian(splits[5], (EXPERTS, D, FF), D ** -0.5, 0.1875, ((0, 16), (1, 2)))
    w_down = gaussian(splits[6], (EXPERTS, D, FF), FF ** -0.5, 0.3125, ((0, 16), (1, 2)))
    return dict(tokens=tokens, grad_out=grad_out, expert_ids=expert_ids, gate_numer=gate_numer, w_gate=w_gate, w_up=w_up, w_down=w_down)


def backward_rows(rows_in, grads_in, gate_mat, up_mat, down_mat):
    pre_gate = jnp.dot(rows_in, gate_mat, preferred_element_type=jnp.float32)
    pre_up = jnp.dot(rows_in, up_mat, preferred_element_type=jnp.float32)
    sigmoid_gate = jax.nn.sigmoid(pre_gate)
    activation = (pre_gate * sigmoid_gate * pre_up).astype(jnp.bfloat16)
    grad_act = jnp.dot(grads_in, down_mat, preferred_element_type=jnp.float32)
    grad_up = (grad_act * pre_gate * sigmoid_gate).astype(jnp.bfloat16)
    grad_gate = (grad_act * pre_up * sigmoid_gate * (1.0 + pre_gate * (1.0 - sigmoid_gate))).astype(jnp.bfloat16)
    grad_rows = jnp.dot(grad_gate, gate_mat.T, preferred_element_type=jnp.float32)
    grad_rows = grad_rows + jnp.dot(grad_up, up_mat.T, preferred_element_type=jnp.float32)
    return grad_rows.astype(jnp.bfloat16), grad_gate, grad_up, activation


def rounded(value):
    return lax.optimization_barrier(value.astype(jnp.bfloat16)).astype(jnp.float32)


def group_tables(flat_ids, group_index):
    pair_count = flat_ids.shape[0]
    sorted_pairs = jnp.argsort(flat_ids, stable=True).astype(jnp.int32)
    expert_range = jnp.arange(EXPERTS, dtype=jnp.int32)
    counts = jnp.sum((flat_ids[:, None] == expert_range[None, :]).astype(jnp.int32), axis=0).astype(jnp.int32)
    starts = (jnp.cumsum(counts) - counts).astype(jnp.int32)
    column = jnp.arange(SLOTS, dtype=jnp.int32)
    is_valid = column[None, :] < counts[:, None]
    position = jnp.minimum(starts[:, None] + column[None, :], pair_count - 1).astype(jnp.int32)
    pair_index = jnp.where(is_valid, sorted_pairs[position], 0).astype(jnp.int32)
    return (pair_index + group_index * pair_count).astype(jnp.int32), is_valid


def reference(tokens, grad_out, expert_ids, gate_numer, w_gate, w_up, w_down):
    numer = gate_numer.astype(jnp.float32)
    gate = (numer / jnp.sum(numer, axis=1, keepdims=True)).reshape(-1)
    group_pairs = GROUP_TOKENS * TOP
    flat_ids = expert_ids.reshape(-1)
    tables = [group_tables(flat_ids[group_index * group_pairs:(group_index + 1) * group_pairs], group_index) for group_index in range(N_DP)]
    pair_table = jnp.stack([entry[0] for entry in tables], axis=1)
    valid_table = jnp.stack([entry[1] for entry in tables], axis=1)

    def per_expert(grad_acc, inputs):
        gate_mat, up_mat, down_mat, pair_rows, valid_rows = inputs
        totals = [jnp.zeros((D, FF), jnp.float32) for _ in range(3)]
        for group_index in range(N_DP):
            pair_index = pair_rows[group_index]
            keep = valid_rows[group_index].astype(jnp.float32)[:, None]
            token_index = (pair_index // TOP).astype(jnp.int32)
            rows_in = (tokens[token_index].astype(jnp.float32) * keep).astype(jnp.bfloat16)
            grads_in = (gate[pair_index][:, None] * grad_out[token_index].astype(jnp.float32) * keep).astype(jnp.bfloat16)
            grad_rows, grad_gate, grad_up, activation = backward_rows(rows_in, grads_in, gate_mat, up_mat, down_mat)
            grad_acc = grad_acc.at[token_index].add(grad_rows.astype(jnp.float32) * keep)
            totals[0] = totals[0] + rounded(jnp.dot(rows_in.T, grad_gate, preferred_element_type=jnp.float32))
            totals[1] = totals[1] + rounded(jnp.dot(rows_in.T, grad_up, preferred_element_type=jnp.float32))
            totals[2] = totals[2] + rounded(jnp.dot(grads_in.T, activation, preferred_element_type=jnp.float32))
        return grad_acc, (totals[0].astype(jnp.bfloat16), totals[1].astype(jnp.bfloat16), totals[2].astype(jnp.bfloat16))

    start_acc = jnp.zeros((TOKENS, D), jnp.float32)
    grad_acc, grads = lax.scan(per_expert, start_acc, (w_gate, w_up, w_down, pair_table, valid_table))
    return grad_acc.astype(jnp.bfloat16), grads[0], grads[1], grads[2]
```

```python
import functools

import jax
import jax.numpy as jnp
from jax import lax
from jax.experimental import pallas as pl
from jax.experimental.pallas import tpu as pltpu
from jax.sharding import PartitionSpec as P

MESH = pl.DeviceIdType.MESH
F32 = jnp.float32
BF16 = jnp.bfloat16


def backward_rows(rows_in, grads_in, gate_mat, up_mat, down_mat):
    pre_gate = jnp.dot(rows_in, gate_mat, preferred_element_type=jnp.float32)
    pre_up = jnp.dot(rows_in, up_mat, preferred_element_type=jnp.float32)
    sigmoid_gate = jax.nn.sigmoid(pre_gate)
    activation = (pre_gate * sigmoid_gate * pre_up).astype(jnp.bfloat16)
    grad_act = jnp.dot(grads_in, down_mat, preferred_element_type=jnp.float32)
    grad_up = (grad_act * pre_gate * sigmoid_gate).astype(jnp.bfloat16)
    grad_gate = (grad_act * pre_up * sigmoid_gate * (1.0 + pre_gate * (1.0 - sigmoid_gate))).astype(
        jnp.bfloat16
    )
    grad_rows = jnp.einsum("rf,df->rd", grad_gate, gate_mat, preferred_element_type=jnp.float32)
    grad_rows = grad_rows + jnp.einsum(
        "rf,df->rd", grad_up, up_mat, preferred_element_type=jnp.float32
    )
    return (grad_rows.astype(jnp.bfloat16), grad_gate, grad_up, activation)


def on_device_routed(tokens, grad_out, expert_ids, gate_numer, w_gate, w_up, w_down):
    peers = lax.axis_size("expert")
    data_groups = lax.axis_size("dp")
    tok_rows = tokens.shape[0]
    model_width = tokens.shape[1]
    top_count = expert_ids.shape[1]
    hidden_width = w_gate.shape[2]
    mean_rows = tok_rows * top_count // peers
    capacity = min(tok_rows, mean_rows + tok_rows * top_count // (8 * peers))
    pair_count = tok_rows * top_count
    slot_count = peers * capacity
    numer = gate_numer.astype(jnp.float32)
    gate = numer / jnp.sum(numer, axis=1, keepdims=True)
    scaled = (gate[:, :, None] * grad_out.astype(jnp.float32)[:, None, :]).astype(jnp.bfloat16)
    scaled = scaled.reshape(pair_count, model_width)
    flat_ids = expert_ids.reshape(-1)
    one_hot = (flat_ids[:, None] == jnp.arange(peers, dtype=jnp.int32)[None, :]).astype(
        jnp.bfloat16
    )
    pair_range = jnp.arange(pair_count, dtype=jnp.int32)
    lower = (pair_range[None, :] < pair_range[:, None]).astype(jnp.bfloat16)
    earlier = jnp.dot(lower, one_hot, preferred_element_type=jnp.float32)
    slot = jnp.sum(earlier * one_hot.astype(jnp.float32), axis=1).astype(jnp.int32)
    target = flat_ids * capacity + slot
    pair_of_slot = jnp.full((slot_count,), pair_count, jnp.int32).at[target].set(pair_range)
    token_of_slot = jnp.where(pair_of_slot < pair_count, pair_of_slot // top_count, tok_rows)
    zero_row = jnp.zeros((1, model_width), jnp.bfloat16)
    padded_tokens = jnp.concatenate([tokens, zero_row], axis=0)
    padded_scaled = jnp.concatenate([scaled, zero_row], axis=0)
    send_rows = padded_tokens[token_of_slot].reshape(peers, capacity, model_width)
    send_grads = padded_scaled[pair_of_slot].reshape(peers, capacity, model_width)
    gathered = (
        lax.all_gather(w_gate, "dp", axis=1, tiled=True),
        lax.all_gather(w_up, "dp", axis=1, tiled=True),
        lax.all_gather(w_down, "dp", axis=1, tiled=True),
    )
    gate_mat = gathered[0][0]
    up_mat = gathered[1][0]
    down_mat = gathered[2][0]
    arrived_rows, arrived_grads = (
        lax.all_to_all(send_rows, "expert", split_axis=0, concat_axis=0, tiled=True),
        lax.all_to_all(send_grads, "expert", split_axis=0, concat_axis=0, tiled=True),
    )
    rows_in = arrived_rows.reshape(slot_count, model_width)
    grads_in = arrived_grads.reshape(slot_count, model_width)
    grad_rows, grad_gate, grad_up, activation = backward_rows(
        rows_in, grads_in, gate_mat, up_mat, down_mat
    )
    returned = lax.all_to_all(
        grad_rows.reshape(peers, capacity, model_width),
        "expert",
        split_axis=0,
        concat_axis=0,
        tiled=True,
    )
    picked = returned.reshape(slot_count, model_width)[target].astype(jnp.float32)
    grad_tokens = jnp.sum(picked.reshape(tok_rows, top_count, model_width), axis=1).astype(
        jnp.bfloat16
    )
    quarter = model_width // data_groups
    term_gate = jnp.einsum(
        "rd,rf->df", rows_in, grad_gate, preferred_element_type=jnp.float32
    ).astype(jnp.bfloat16)
    term_up = jnp.einsum("rd,rf->df", rows_in, grad_up, preferred_element_type=jnp.float32).astype(
        jnp.bfloat16
    )
    term_down = jnp.einsum(
        "rd,rf->df", grads_in, activation, preferred_element_type=jnp.float32
    ).astype(jnp.bfloat16)
    stacked = jnp.stack([term_gate, term_up, term_down]).reshape(
        3, data_groups, quarter, hidden_width
    )
    arrived = lax.all_to_all(stacked, "dp", split_axis=1, concat_axis=1, tiled=True)
    summed = jnp.sum(arrived.astype(jnp.float32), axis=1).astype(jnp.bfloat16)
    return (grad_tokens, summed[0][None], summed[1][None], summed[2][None])


def contract_rows(lhs, rhs):
    return lax.dot_general(lhs, rhs, (((0,), (0,)), ((), ())), preferred_element_type=F32)


def layer_kernel(
    chips, tok_ref, grad_ref, num_ref, wg_ref, wu_ref, wd_ref,
    out_tok, out_gate, out_up, out_down,
    xbuf, gbuf, nbuf, cbuf, sbuf, obuf, rbuf, wgu, wdn, acc_gu, acc_d, pbuf, qbuf, scaled, grads,
    w_send, w_recv, ring_send, ring_recv, sib_send, sib_recv,
    row_send, row_recv, sum_send, sum_recv, part_send, part_recv,
):
    half_ring = chips // 2
    group = lax.axis_index("dp")
    me = lax.axis_index("expert")
    core = lax.rem(me, 2)
    chip = lax.div(me, 2)
    lane = lax.rem(chip, 2)
    depth = lax.div(chip, 2)
    pos = jnp.where(lane == 0, depth, chips - 1 - depth)

    def device_at(ring_pos):
        far = ring_pos >= half_ring
        along = jnp.where(far, chips - 1 - ring_pos, ring_pos)
        return along * 4 + jnp.where(far, 2, 0) + core

    def ring(offset):
        return lax.rem(pos + offset + chips, chips)

    right = (group, device_at(ring(1)))
    left = (group, device_at(ring(-1)))
    sibling = (group, me + 1 - 2 * core)
    other = (1 - group, me)
    flows = (right, left)

    barrier = pltpu.get_barrier_semaphore()
    for target in (right, left, sibling, other):
        pl.semaphore_signal(barrier, inc=1, device_id=target, device_id_type=MESH)
    pl.semaphore_wait(barrier, 4)

    started = []

    def copy(src, dst, send, recv, target):
        return pltpu.make_async_remote_copy(
            src_ref=src, dst_ref=dst, send_sem=send, recv_sem=recv,
            device_id=target, device_id_type=MESH,
        )

    def start(*args):
        op = copy(*args)
        op.start()
        started.append(op)

    share = wg_ref.shape[0]
    hidden = wg_ref.shape[1]
    own_rows = pl.ds(pl.multiple_of(group * share, share), share)
    other_rows = pl.ds(pl.multiple_of((1 - group) * share, share), share)

    own = (tok_ref, grad_ref, num_ref)
    bufs = (xbuf, gbuf, nbuf)

    def weight_places(rows):
        return (
            wgu.at[rows, pl.ds(0, hidden)],
            wgu.at[rows, pl.ds(hidden, hidden)],
            wdn.at[rows, :],
        )

    for a in (0, 2, 1):
        for f in range(2):
            start(own[a], bufs[a].at[pos, core], ring_send.at[a, f, 0], ring_recv.at[a, f, 0], flows[f])
    for k, ref in enumerate((wg_ref, wu_ref, wd_ref)):
        start(ref, weight_places(own_rows)[k], w_send.at[k], w_recv.at[k], other)
    for a in (0, 2, 1):
        start(own[a], bufs[a].at[pos, core], sib_send.at[a, 0], sib_recv.at[a, 0], sibling)
    for a in range(3):
        bufs[a][pos, core] = own[a][...]
    wgu[own_rows, pl.ds(0, hidden)] = wg_ref[...]
    wgu[own_rows, pl.ds(hidden, hidden)] = wu_ref[...]
    wdn[own_rows, :] = wd_ref[...]
    acc_gu[...] = jnp.zeros_like(acc_gu)
    acc_d[...] = jnp.zeros_like(acc_d)

    def part(a, q, c, step, f):
        ref = bufs[a].at[q, c]
        if step == half_ring:
            n = bufs[a].shape[2] // 2
            ref = bufs[a].at[q, c, pl.ds(f * n, n)]
        return ref

    def arrive(a, step):
        for f in range(2):
            q = ring(-step if f == 0 else step)
            ref = part(a, q, core, step, f)
            copy(ref, ref, ring_send.at[a, f, step - 1], ring_recv.at[a, f, step - 1], flows[f]).wait_recv()
            if step < half_ring:
                ref2 = part(a, q, core, step + 1, f)
                start(ref2, ref2, ring_send.at[a, f, step], ring_recv.at[a, f, step], flows[f])
            k = 2 * step - 1 + f
            start(ref, ref, sib_send.at[a, k], sib_recv.at[a, k], sibling)

    def arrive_sibling(step):
        for a in range(3):
            for f in range(2 if step else 1):
                q = ring(-step if f == 0 else step)
                ref = part(a, q, 1 - core, step, f)
                k = 2 * step - 1 + f if step else 0
                copy(ref, ref, sib_send.at[a, k], sib_recv.at[a, k], sibling).wait_recv()

    rows = 2 * tok_ref.shape[0]
    width = tok_ref.shape[1]
    block = tok_ref.shape[0]
    experts = num_ref.shape[0] // 2
    row_ids = lax.broadcasted_iota(jnp.int32, (2 * experts, 256), 0)
    col_ids = lax.broadcasted_iota(jnp.int32, (2 * experts, 256), 1)
    wanted = jnp.where(col_ids < 128, me, experts)
    select = jnp.where(row_ids == wanted, 1.0, 0.0).astype(BF16)

    def chunk_ring(i):
        return lax.rem(pos + (1 - 2 * (i % 2)) * ((i + 1) // 2) + chips, chips)

    def chunk(i, carry):
        away = lax.div(i + 1, 2)
        q = lax.rem(pos + (1 - 2 * lax.rem(i, 2)) * away + chips, chips)
        for b in range(2):
            both = contract_rows(nbuf[q, b], select)
            gate = both[:, :128] / both[:, 128:]
            for k in range(width // 128):
                cols = pl.ds(k * 128, 128)
                scaled[pl.ds(b * block, block), cols] = (
                    gate * gbuf[q, b, :, cols].astype(F32)
                ).astype(BF16)
        x = xbuf[q].reshape(rows, width)
        pre = jnp.dot(x, wgu[...], preferred_element_type=F32)
        pre_gate = pre[:, :hidden]
        pre_up = pre[:, hidden:]
        grad_act = jnp.dot(scaled[...], wdn[...], preferred_element_type=F32)
        sig = jax.nn.sigmoid(pre_gate)
        silu = pre_gate * sig
        act = (silu * pre_up).astype(BF16)
        grads[:, pl.ds(hidden, hidden)] = (grad_act * silu).astype(BF16)
        grads[:, pl.ds(0, hidden)] = (
            grad_act * pre_up * sig * (1.0 + pre_gate * (1.0 - sig))
        ).astype(BF16)
        back = lax.dot_general(
            grads[...], wgu[...], (((1,), (1,)), ((), ())), preferred_element_type=F32
        )
        cbuf[q] = back.astype(BF16).reshape(2, block, width)
        acc_gu[...] += contract_rows(x, grads[...])
        acc_d[...] += contract_rows(scaled[...], act)
        return carry

    def chunks(first, last):
        lax.fori_loop(first, last, chunk, 0)
        for i in range(first, last):
            q = chunk_ring(i)
            start(cbuf.at[q, 1 - core], sbuf.at[q], row_send.at[i], row_recv.at[i], sibling)

    for step in range(1, half_ring - 1):
        for a in (0, 2, 1):
            arrive(a, step)
    for k, ref in enumerate(weight_places(other_rows)):
        copy(ref, ref, w_send.at[k], w_recv.at[k], other).wait_recv()
    for step in range(half_ring - 1):
        arrive_sibling(step)
    chunks(0, 3)
    arrive(0, half_ring - 1)
    chunks(3, 4)
    arrive(2, half_ring - 1)
    arrive(1, half_ring - 1)
    arrive_sibling(half_ring - 1)
    chunks(4, 7)
    for a in (0, 2, 1):
        arrive(a, half_ring)
    arrive_sibling(half_ring)
    chunks(7, 8)

    def term(k, where):
        if k == 2:
            return acc_d[where, :].astype(BF16)
        return acc_gu[where, pl.ds(k * hidden, hidden)].astype(BF16)

    for k in range(3):
        pbuf[k] = term(k, other_rows)
        start(pbuf.at[k], qbuf.at[k], part_send.at[k], part_recv.at[k], other)

    half = block // 2
    got_rows = set()

    def row_sum(q_off, h):
        off = q_off
        i = 0 if off == 0 else (2 * off if off > 0 else -2 * off - 1)
        i = min(i, chips - 1)
        q = ring(off)
        if i not in got_rows:
            got_rows.add(i)
            copy(sbuf.at[q], sbuf.at[q], row_send.at[i], row_recv.at[i], sibling).wait_recv()
        at = pl.ds(h * half, half)
        return cbuf[q, core, at].astype(F32) + sbuf[q, at].astype(F32)

    def order(f):
        listed = [(half_ring, f)]
        for d in range(half_ring - 1, 0, -1):
            listed += [(d, 1 - f), (d, f)]
        return listed

    def incoming(f, d, h):
        j = order(f).index((d + 1, h))
        ref = rbuf.at[f, j]
        copy(ref, ref, sum_send.at[f, j], sum_recv.at[f, j], flows[f]).wait_recv()
        return rbuf[f, j].astype(F32)

    for j in range(len(order(0))):
        for f in range(2):
            d, h = order(f)[j]
            value = row_sum(d if f == 0 else -d, h)
            if (d + 1, h) in order(f):
                value = value + incoming(f, d, h)
            obuf[f, j] = value.astype(BF16)
            start(obuf.at[f, j], rbuf.at[f, j], sum_send.at[f, j], sum_recv.at[f, j], flows[f])
    for h in range(2):
        value = row_sum(0, h) + incoming(0, 0, h) + incoming(1, 0, h)
        out_tok[pl.ds(h * half, half), :] = value.astype(BF16)

    for k, out in enumerate((out_gate, out_up, out_down)):
        copy(qbuf.at[k], qbuf.at[k], part_send.at[k], part_recv.at[k], other).wait_recv()
        out[...] = (term(k, own_rows).astype(F32) + qbuf[k].astype(F32)).astype(BF16)
    for op in started:
        op.wait_send()


def on_device_dense(tokens, grad_out, expert_ids, gate_numer, w_gate, w_up, w_down):
    peers = lax.axis_size("expert")
    chips = peers // 2
    block, width = tokens.shape
    share, hidden = w_gate.shape[1:]
    depth = share * lax.axis_size("dp")
    hit = expert_ids.T[None, :, :] == jnp.arange(peers, dtype=jnp.int32)[:, None, None]
    by_expert = jnp.sum(jnp.where(hit, gate_numer.T[None], 0), axis=1)
    total = jnp.broadcast_to(jnp.sum(gate_numer, axis=1)[None, :], (peers, block))
    numbers = jnp.concatenate([by_expert, total], axis=0).astype(BF16)

    messages = chips - 1
    dma = pltpu.SemaphoreType.DMA
    vmem = pl.BlockSpec(memory_space=pltpu.VMEM)
    outs = pl.pallas_call(
        functools.partial(layer_kernel, chips),
        out_shape=(jax.ShapeDtypeStruct((block, width), BF16),)
        + (jax.ShapeDtypeStruct((share, hidden), BF16),) * 3,
        in_specs=[vmem] * 6,
        out_specs=(vmem,) * 4,
        scratch_shapes=[
            pltpu.VMEM((chips, 2, block, width), BF16),
            pltpu.VMEM((chips, 2, block, width), BF16),
            pltpu.VMEM((chips, 2, 2 * peers, block), BF16),
            pltpu.VMEM((chips, 2, block, width), BF16),
            pltpu.VMEM((chips, block, width), BF16),
            pltpu.VMEM((2, messages, block // 2, width), BF16),
            pltpu.VMEM((2, messages, block // 2, width), BF16),
            pltpu.VMEM((depth, 2 * hidden), BF16),
            pltpu.VMEM((depth, hidden), BF16),
            pltpu.VMEM((depth, 2 * hidden), F32),
            pltpu.VMEM((depth, hidden), F32),
            pltpu.VMEM((3, share, hidden), BF16),
            pltpu.VMEM((3, share, hidden), BF16),
            pltpu.VMEM((2 * block, width), BF16),
            pltpu.VMEM((2 * block, 2 * hidden), BF16),
            dma((3,)), dma((3,)),
            dma((3, 2, chips // 2)), dma((3, 2, chips // 2)),
            dma((3, chips + 1)), dma((3, chips + 1)),
            dma((chips,)), dma((chips,)),
            dma((2, messages)), dma((2, messages)),
            dma((3,)), dma((3,)),
        ],
        compiler_params=pltpu.CompilerParams(
            collective_id=0, has_side_effects=True, vmem_limit_bytes=56 * 1024 * 1024
        ),
        cost_estimate=pl.CostEstimate(
            flops=16 * peers * block * width * hidden, bytes_accessed=8 * block * width, transcendentals=0
        ),
    )(tokens, grad_out, numbers, w_gate[0], w_up[0], w_down[0])
    return (outs[0],) + tuple(value[None] for value in outs[1:])


def solution(mesh):
    return jax.shard_map(
        on_device_dense if mesh.shape["expert"] == 16 else on_device_routed,
        mesh=mesh,
        in_specs=(
            P(("dp", "expert"), None),
            P(("dp", "expert"), None),
            P(("dp", "expert"), None),
            P(("dp", "expert"), None),
            P("expert", "dp", None),
            P("expert", "dp", None),
            P("expert", "dp", None),
        ),
        out_specs=(
            P(("dp", "expert"), None),
            P("expert", "dp", None),
            P("expert", "dp", None),
            P("expert", "dp", None),
        ),
        check_vma=False,
    )
```

```python
import functools

import jax
import jax.numpy as jnp
from jax import lax
from jax.experimental import pallas as pl
from jax.experimental.pallas import tpu as pltpu
from jax.sharding import PartitionSpec as P

MESH = pl.DeviceIdType.MESH
F32 = jnp.float32
BF16 = jnp.bfloat16


def backward_rows(rows_in, grads_in, gate_mat, up_mat, down_mat):
    pre_gate = jnp.dot(rows_in, gate_mat, preferred_element_type=jnp.float32)
    pre_up = jnp.dot(rows_in, up_mat, preferred_element_type=jnp.float32)
    sigmoid_gate = jax.nn.sigmoid(pre_gate)
    activation = (pre_gate * sigmoid_gate * pre_up).astype(jnp.bfloat16)
    grad_act = jnp.dot(grads_in, down_mat, preferred_element_type=jnp.float32)
    grad_up = (grad_act * pre_gate * sigmoid_gate).astype(jnp.bfloat16)
    grad_gate = (grad_act * pre_up * sigmoid_gate * (1.0 + pre_gate * (1.0 - sigmoid_gate))).astype(
        jnp.bfloat16
    )
    grad_rows = jnp.einsum("rf,df->rd", grad_gate, gate_mat, preferred_element_type=jnp.float32)
    grad_rows = grad_rows + jnp.einsum(
        "rf,df->rd", grad_up, up_mat, preferred_element_type=jnp.float32
    )
    return (grad_rows.astype(jnp.bfloat16), grad_gate, grad_up, activation)


def on_device_routed(tokens, grad_out, expert_ids, gate_numer, w_gate, w_up, w_down):
    peers = lax.axis_size("expert")
    data_groups = lax.axis_size("dp")
    tok_rows = tokens.shape[0]
    model_width = tokens.shape[1]
    top_count = expert_ids.shape[1]
    hidden_width = w_gate.shape[2]
    mean_rows = tok_rows * top_count // peers
    capacity = min(tok_rows, mean_rows + tok_rows * top_count // (8 * peers))
    pair_count = tok_rows * top_count
    slot_count = peers * capacity
    numer = gate_numer.astype(jnp.float32)
    gate = numer / jnp.sum(numer, axis=1, keepdims=True)
    scaled = (gate[:, :, None] * grad_out.astype(jnp.float32)[:, None, :]).astype(jnp.bfloat16)
    scaled = scaled.reshape(pair_count, model_width)
    flat_ids = expert_ids.reshape(-1)
    one_hot = (flat_ids[:, None] == jnp.arange(peers, dtype=jnp.int32)[None, :]).astype(
        jnp.bfloat16
    )
    pair_range = jnp.arange(pair_count, dtype=jnp.int32)
    lower = (pair_range[None, :] < pair_range[:, None]).astype(jnp.bfloat16)
    earlier = jnp.dot(lower, one_hot, preferred_element_type=jnp.float32)
    slot = jnp.sum(earlier * one_hot.astype(jnp.float32), axis=1).astype(jnp.int32)
    target = flat_ids * capacity + slot
    pair_of_slot = jnp.full((slot_count,), pair_count, jnp.int32).at[target].set(pair_range)
    token_of_slot = jnp.where(pair_of_slot < pair_count, pair_of_slot // top_count, tok_rows)
    zero_row = jnp.zeros((1, model_width), jnp.bfloat16)
    padded_tokens = jnp.concatenate([tokens, zero_row], axis=0)
    padded_scaled = jnp.concatenate([scaled, zero_row], axis=0)
    send_rows = padded_tokens[token_of_slot].reshape(peers, capacity, model_width)
    send_grads = padded_scaled[pair_of_slot].reshape(peers, capacity, model_width)
    gathered = (
        lax.all_gather(w_gate, "dp", axis=1, tiled=True),
        lax.all_gather(w_up, "dp", axis=1, tiled=True),
        lax.all_gather(w_down, "dp", axis=1, tiled=True),
    )
    gate_mat = gathered[0][0]
    up_mat = gathered[1][0]
    down_mat = gathered[2][0]
    arrived_rows, arrived_grads = (
        lax.all_to_all(send_rows, "expert", split_axis=0, concat_axis=0, tiled=True),
        lax.all_to_all(send_grads, "expert", split_axis=0, concat_axis=0, tiled=True),
    )
    rows_in = arrived_rows.reshape(slot_count, model_width)
    grads_in = arrived_grads.reshape(slot_count, model_width)
    grad_rows, grad_gate, grad_up, activation = backward_rows(
        rows_in, grads_in, gate_mat, up_mat, down_mat
    )
    returned = lax.all_to_all(
        grad_rows.reshape(peers, capacity, model_width),
        "expert",
        split_axis=0,
        concat_axis=0,
        tiled=True,
    )
    picked = returned.reshape(slot_count, model_width)[target].astype(jnp.float32)
    grad_tokens = jnp.sum(picked.reshape(tok_rows, top_count, model_width), axis=1).astype(
        jnp.bfloat16
    )
    quarter = model_width // data_groups
    term_gate = jnp.einsum(
        "rd,rf->df", rows_in, grad_gate, preferred_element_type=jnp.float32
    ).astype(jnp.bfloat16)
    term_up = jnp.einsum("rd,rf->df", rows_in, grad_up, preferred_element_type=jnp.float32).astype(
        jnp.bfloat16
    )
    term_down = jnp.einsum(
        "rd,rf->df", grads_in, activation, preferred_element_type=jnp.float32
    ).astype(jnp.bfloat16)
    stacked = jnp.stack([term_gate, term_up, term_down]).reshape(
        3, data_groups, quarter, hidden_width
    )
    arrived = lax.all_to_all(stacked, "dp", split_axis=1, concat_axis=1, tiled=True)
    summed = jnp.sum(arrived.astype(jnp.float32), axis=1).astype(jnp.bfloat16)
    return (grad_tokens, summed[0][None], summed[1][None], summed[2][None])


def contract_rows(lhs, rhs):
    return lax.dot_general(lhs, rhs, (((0,), (0,)), ((), ())), preferred_element_type=F32)


def layer_kernel(
    chips, tok_ref, grad_ref, num_ref, wg_ref, wu_ref, wd_ref,
    out_tok, out_gate, out_up, out_down,
    xbuf, gbuf, nbuf, cbuf, sbuf, obuf, rbuf, wgu, wdn, acc_gu, acc_d, pbuf, qbuf, scaled, grads, acts,
    pre_buf, ga_buf,
    w_send, w_recv, ring_send, ring_recv, sib_send, sib_recv,
    row_send, row_recv, sum_send, sum_recv, part_send, part_recv,
):
    half_ring = chips // 2
    group = lax.axis_index("dp")
    me = lax.axis_index("expert")
    core = lax.rem(me, 2)
    chip = lax.div(me, 2)
    lane = lax.rem(chip, 2)
    depth = lax.div(chip, 2)
    pos = jnp.where(lane == 0, depth, chips - 1 - depth)

    def device_at(ring_pos):
        far = ring_pos >= half_ring
        along = jnp.where(far, chips - 1 - ring_pos, ring_pos)
        return along * 4 + jnp.where(far, 2, 0) + core

    def ring(offset):
        return lax.rem(pos + offset + chips, chips)

    right = (group, device_at(ring(1)))
    left = (group, device_at(ring(-1)))
    sibling = (group, me + 1 - 2 * core)
    other = (1 - group, me)
    flows = (right, left)

    barrier = pltpu.get_barrier_semaphore()
    for target in (right, left, sibling, other):
        pl.semaphore_signal(barrier, inc=1, device_id=target, device_id_type=MESH)
    pl.semaphore_wait(barrier, 4)

    started = []

    def copy(src, dst, send, recv, target):
        return pltpu.make_async_remote_copy(
            src_ref=src, dst_ref=dst, send_sem=send, recv_sem=recv,
            device_id=target, device_id_type=MESH,
        )

    def start(*args):
        op = copy(*args)
        op.start()
        started.append(op)

    share = wg_ref.shape[0]
    hidden = wg_ref.shape[1]
    block, width = tok_ref.shape
    own_at = pl.ds(pl.multiple_of(group * share, share), share)
    other_at = pl.ds(pl.multiple_of((1 - group) * share, share), share)

    def slot(f, d):
        return 0 if d == 0 else min(2 * d - 1 + f, chips - 1)

    own = (tok_ref, grad_ref, num_ref)
    bufs = (xbuf, gbuf, nbuf)

    def weight_places(rows):
        return (
            wgu.at[rows, pl.ds(0, hidden)],
            wgu.at[rows, pl.ds(hidden, hidden)],
            wdn.at[rows, :],
        )

    for a in (0, 2, 1):
        for f in range(2):
            start(own[a], bufs[a].at[slot(f, 1), core], ring_send.at[a, f, 0], ring_recv.at[a, f, 0], flows[f])
    for k, ref in enumerate((wg_ref, wu_ref, wd_ref)):
        start(ref, weight_places(own_at)[k], w_send.at[k], w_recv.at[k], other)
    for a in (0, 2, 1):
        start(own[a], bufs[a].at[0, core], sib_send.at[a, 0], sib_recv.at[a, 0], sibling)
    for a in range(3):
        bufs[a][0, core] = own[a][...]
    wgu[own_at, pl.ds(0, hidden)] = wg_ref[...]
    wgu[own_at, pl.ds(hidden, hidden)] = wu_ref[...]
    wdn[own_at, :] = wd_ref[...]

    def part(a, s, c, step, f):
        if step == half_ring:
            n = bufs[a].shape[2] // 2
            return bufs[a].at[s, c, pl.ds(f * n, n)]
        return bufs[a].at[s, c]

    def arrive(a, step):
        for f in range(2):
            ref = part(a, slot(f, step), core, step, f)
            copy(ref, ref, ring_send.at[a, f, step - 1], ring_recv.at[a, f, step - 1], flows[f]).wait_recv()
            if step < half_ring:
                src = part(a, slot(f, step), core, step + 1, f)
                dst = part(a, slot(f, step + 1), core, step + 1, f)
                start(src, dst, ring_send.at[a, f, step], ring_recv.at[a, f, step], flows[f])
            k = 2 * step - 1 + f
            start(ref, ref, sib_send.at[a, k], sib_recv.at[a, k], sibling)

    def arrive_sibling(step, arrays=(0, 1, 2)):
        for a in arrays:
            for f in range(2 if step else 1):
                ref = part(a, slot(f, step), 1 - core, step, f)
                k = 2 * step - 1 + f if step else 0
                copy(ref, ref, sib_send.at[a, k], sib_recv.at[a, k], sibling).wait_recv()

    per_slot = 2 * block
    experts = num_ref.shape[0] // 2
    row_ids = lax.broadcasted_iota(jnp.int32, (2 * experts, 256), 0)
    col_ids = lax.broadcasted_iota(jnp.int32, (2 * experts, 256), 1)
    wanted = jnp.where(col_ids < 128, me, experts)
    select = jnp.where(row_ids == wanted, 1.0, 0.0).astype(BF16)

    def span(slots):
        return pl.ds(slots[0] * per_slot, len(slots) * per_slot)

    def tokens_of(slots, cols=slice(None)):
        return xbuf[slots[0] : slots[-1] + 1, :, :, cols].reshape(len(slots) * per_slot, -1)

    def scale(slots):
        for s in slots:
            for b in range(2):
                both = contract_rows(nbuf[s, b], select)
                gate = both[:, :128] / both[:, 128:]
                for k in range(width // 128):
                    cols = pl.ds(k * 128, 128)
                    scaled[pl.ds(s * per_slot + b * block, block), cols] = (
                        gate * gbuf[s, b, :, cols].astype(F32)
                    ).astype(BF16)

    def pre_part(slots, at):
        x = tokens_of(slots, at)
        return jnp.dot(x, wgu[at, :], preferred_element_type=F32)

    def ga_part(slots, at):
        return jnp.dot(scaled[span(slots), at], wdn[at, :], preferred_element_type=F32)

    def pointwise(slots, pre, grad_act):
        where = span(slots)
        pre_gate = pre[:, :hidden]
        pre_up = pre[:, hidden:]
        sig = jax.nn.sigmoid(pre_gate)
        silu = pre_gate * sig
        acts[where, :] = (silu * pre_up).astype(BF16)
        grads[where, pl.ds(hidden, hidden)] = (grad_act * silu).astype(BF16)
        grads[where, pl.ds(0, hidden)] = (
            grad_act * pre_up * sig * (1.0 + pre_gate * (1.0 - sig))
        ).astype(BF16)

    def back(slots):
        rows = lax.dot_general(
            grads[span(slots), :], wgu[...], (((1,), (1,)), ((), ())), preferred_element_type=F32
        )
        cbuf[slots[0] : slots[-1] + 1] = rows.astype(BF16).reshape(len(slots), 2, block, width)
        for s in slots:
            start(cbuf.at[s, 1 - core], sbuf.at[s], row_send.at[s], row_recv.at[s], sibling)

    def add_terms(slots, first=False):
        where = span(slots)
        gu = contract_rows(tokens_of(slots, other_at), grads[where, :])
        dn = contract_rows(scaled[where, other_at], acts[where, :])
        if first:
            acc_gu[...] = gu
            acc_d[...] = dn
        else:
            acc_gu[...] += gu
            acc_d[...] += dn

    def rest(slots, first=False):
        pointwise(slots, pre_buf[span(slots), :], ga_buf[span(slots), :])
        back(slots)
        add_terms(slots, first)

    def wait_weight(k):
        ref = weight_places(other_at)[k]
        copy(ref, ref, w_send.at[k], w_recv.at[k], other).wait_recv()

    slots_a, slots_b, slots_c, slots_d, slots_e = [0], [1, 2], [3, 4], [5, 6], [7]
    everything = slice(None)

    arrive_sibling(0)
    scale(slots_a)
    pre_buf[span(slots_a), :] = pre_part(slots_a, own_at)
    ga_buf[span(slots_a), :] = ga_part(slots_a, own_at)
    arrive(0, 1)
    arrive_sibling(1, (0,))
    pre_buf[span(slots_b), :] = pre_part(slots_b, own_at)
    arrive(2, 1)
    arrive(1, 1)
    arrive_sibling(1, (1, 2))
    scale(slots_b)
    ga_buf[span(slots_b), :] = ga_part(slots_b, own_at)
    arrive(0, 2)
    arrive_sibling(2, (0,))
    wait_weight(0)
    wait_weight(1)
    pre_buf[span(slots_a), :] += pre_part(slots_a, other_at)
    pre_buf[span(slots_b), :] += pre_part(slots_b, other_at)
    arrive(2, 2)
    arrive(1, 2)
    pre_buf[span(slots_c), :] = pre_part(slots_c, everything)
    wait_weight(2)
    ga_buf[span(slots_a), :] += ga_part(slots_a, other_at)
    rest(slots_a, True)
    ga_buf[span(slots_b), :] += ga_part(slots_b, other_at)
    arrive(0, 3)
    rest(slots_b)
    arrive_sibling(2, (1, 2))
    scale(slots_c)
    ga_buf[span(slots_c), :] = ga_part(slots_c, everything)
    arrive(2, 3)
    arrive(1, 3)
    rest(slots_c)
    arrive_sibling(3)
    scale(slots_d)
    pointwise(slots_d, pre_part(slots_d, everything), ga_part(slots_d, everything))
    for a in (0, 2, 1):
        arrive(a, 4)
    back(slots_d)
    add_terms(slots_d)
    arrive_sibling(4)
    scale(slots_e)
    pointwise(slots_e, pre_part(slots_e, everything), ga_part(slots_e, everything))
    back(slots_e)

    last = span(slots_e)
    for k in range(3):
        if k == 2:
            value = acc_d[...] + contract_rows(scaled[last, other_at], acts[last, :])
        else:
            cols = pl.ds(k * hidden, hidden)
            value = acc_gu[:, cols] + contract_rows(tokens_of(slots_e, other_at), grads[last, cols])
        pbuf[k] = value.astype(BF16)
        start(pbuf.at[k], qbuf.at[k], part_send.at[k], part_recv.at[k], other)

    half = block // 2
    got_rows = set()

    def row_sum(s, h):
        if s not in got_rows:
            got_rows.add(s)
            copy(sbuf.at[s], sbuf.at[s], row_send.at[s], row_recv.at[s], sibling).wait_recv()
        at = pl.ds(h * half, half)
        return cbuf[s, core, at].astype(F32) + sbuf[s, at].astype(F32)

    def order(f):
        listed = [(half_ring, f)]
        for d in range(half_ring - 1, 0, -1):
            listed += [(d, 1 - f), (d, f)]
        return listed

    def incoming(f, d, h):
        j = order(f).index((d + 1, h))
        ref = rbuf.at[f, j]
        copy(ref, ref, sum_send.at[f, j], sum_recv.at[f, j], flows[f]).wait_recv()
        return rbuf[f, j].astype(F32)

    outs = (out_gate, out_up, out_down)

    def own_term(k):
        if k == 2:
            value = contract_rows(scaled[:, own_at], acts[...])
        else:
            value = contract_rows(
                tokens_of(list(range(chips)), own_at), grads[:, pl.ds(k * hidden, hidden)]
            )
        outs[k][...] = value.astype(BF16)

    for j in range(len(order(0))):
        for f in range(2):
            d, h = order(f)[j]
            value = row_sum(slot(1 - f, d), h)
            if (d + 1, h) in order(f):
                value = value + incoming(f, d, h)
            obuf[f, j] = value.astype(BF16)
            start(obuf.at[f, j], rbuf.at[f, j], sum_send.at[f, j], sum_recv.at[f, j], flows[f])
        if 1 <= j <= 3:
            own_term(j - 1)
    for h in range(2):
        value = row_sum(0, h) + incoming(0, 0, h) + incoming(1, 0, h)
        out_tok[pl.ds(h * half, half), :] = value.astype(BF16)

    for k, out in enumerate(outs):
        copy(qbuf.at[k], qbuf.at[k], part_send.at[k], part_recv.at[k], other).wait_recv()
        out[...] = (out[...].astype(F32) + qbuf[k].astype(F32)).astype(BF16)
    for op in started:
        op.wait_send()


def on_device_dense(tokens, grad_out, expert_ids, gate_numer, w_gate, w_up, w_down):
    peers = lax.axis_size("expert")
    chips = peers // 2
    block, width = tokens.shape
    share, hidden = w_gate.shape[1:]
    depth = share * lax.axis_size("dp")
    hit = expert_ids.T[None, :, :] == jnp.arange(peers, dtype=jnp.int32)[:, None, None]
    by_expert = jnp.sum(jnp.where(hit, gate_numer.T[None], 0), axis=1)
    total = jnp.broadcast_to(jnp.sum(gate_numer, axis=1)[None, :], (peers, block))
    numbers = jnp.concatenate([by_expert, total], axis=0).astype(BF16)

    messages = chips - 1
    rows = peers * block
    early = (chips - 3) * 2 * block
    dma = pltpu.SemaphoreType.DMA
    vmem = pl.BlockSpec(memory_space=pltpu.VMEM)
    outs = pl.pallas_call(
        functools.partial(layer_kernel, chips),
        out_shape=(jax.ShapeDtypeStruct((block, width), BF16),)
        + (jax.ShapeDtypeStruct((share, hidden), BF16),) * 3,
        in_specs=[vmem] * 6,
        out_specs=(vmem,) * 4,
        scratch_shapes=[
            pltpu.VMEM((chips, 2, block, width), BF16),
            pltpu.VMEM((chips, 2, block, width), BF16),
            pltpu.VMEM((chips, 2, 2 * peers, block), BF16),
            pltpu.VMEM((chips, 2, block, width), BF16),
            pltpu.VMEM((chips, block, width), BF16),
            pltpu.VMEM((2, messages, block // 2, width), BF16),
            pltpu.VMEM((2, messages, block // 2, width), BF16),
            pltpu.VMEM((depth, 2 * hidden), BF16),
            pltpu.VMEM((depth, hidden), BF16),
            pltpu.VMEM((share, 2 * hidden), F32),
            pltpu.VMEM((share, hidden), F32),
            pltpu.VMEM((3, share, hidden), BF16),
            pltpu.VMEM((3, share, hidden), BF16),
            pltpu.VMEM((rows, width), BF16),
            pltpu.VMEM((rows, 2 * hidden), BF16),
            pltpu.VMEM((rows, hidden), BF16),
            pltpu.VMEM((early, 2 * hidden), F32),
            pltpu.VMEM((early, hidden), F32),
            dma((3,)), dma((3,)),
            dma((3, 2, chips // 2)), dma((3, 2, chips // 2)),
            dma((3, chips + 1)), dma((3, chips + 1)),
            dma((chips,)), dma((chips,)),
            dma((2, messages)), dma((2, messages)),
            dma((3,)), dma((3,)),
        ],
        compiler_params=pltpu.CompilerParams(
            collective_id=0, has_side_effects=True, vmem_limit_bytes=58 * 1024 * 1024
        ),
        cost_estimate=pl.CostEstimate(
            flops=16 * peers * block * width * hidden, bytes_accessed=8 * block * width, transcendentals=0
        ),
    )(tokens, grad_out, numbers, w_gate[0], w_up[0], w_down[0])
    return (outs[0],) + tuple(value[None] for value in outs[1:])


def solution(mesh):
    return jax.shard_map(
        on_device_dense if mesh.shape["expert"] == 16 else on_device_routed,
        mesh=mesh,
        in_specs=(
            P(("dp", "expert"), None),
            P(("dp", "expert"), None),
            P(("dp", "expert"), None),
            P(("dp", "expert"), None),
            P("expert", "dp", None),
            P("expert", "dp", None),
            P("expert", "dp", None),
        ),
        out_specs=(
            P(("dp", "expert"), None),
            P("expert", "dp", None),
            P("expert", "dp", None),
            P("expert", "dp", None),
        ),
        check_vma=False,
    )
```

```python
import functools

import jax
import jax.numpy as jnp
from jax import lax
from jax.experimental import pallas as pl
from jax.experimental.pallas import tpu as pltpu
from jax.sharding import PartitionSpec as P

MESH = pl.DeviceIdType.MESH
F32 = jnp.float32
BF16 = jnp.bfloat16


def backward_rows(rows_in, grads_in, gate_mat, up_mat, down_mat):
    pre_gate = jnp.dot(rows_in, gate_mat, preferred_element_type=jnp.float32)
    pre_up = jnp.dot(rows_in, up_mat, preferred_element_type=jnp.float32)
    sigmoid_gate = jax.nn.sigmoid(pre_gate)
    activation = (pre_gate * sigmoid_gate * pre_up).astype(jnp.bfloat16)
    grad_act = jnp.dot(grads_in, down_mat, preferred_element_type=jnp.float32)
    grad_up = (grad_act * pre_gate * sigmoid_gate).astype(jnp.bfloat16)
    grad_gate = (grad_act * pre_up * sigmoid_gate * (1.0 + pre_gate * (1.0 - sigmoid_gate))).astype(
        jnp.bfloat16
    )
    grad_rows = jnp.einsum("rf,df->rd", grad_gate, gate_mat, preferred_element_type=jnp.float32)
    grad_rows = grad_rows + jnp.einsum(
        "rf,df->rd", grad_up, up_mat, preferred_element_type=jnp.float32
    )
    return (grad_rows.astype(jnp.bfloat16), grad_gate, grad_up, activation)


def on_device_routed(tokens, grad_out, expert_ids, gate_numer, w_gate, w_up, w_down):
    peers = lax.axis_size("expert")
    data_groups = lax.axis_size("dp")
    tok_rows = tokens.shape[0]
    model_width = tokens.shape[1]
    top_count = expert_ids.shape[1]
    hidden_width = w_gate.shape[2]
    mean_rows = tok_rows * top_count // peers
    capacity = min(tok_rows, mean_rows + tok_rows * top_count // (8 * peers))
    pair_count = tok_rows * top_count
    slot_count = peers * capacity
    numer = gate_numer.astype(jnp.float32)
    gate = numer / jnp.sum(numer, axis=1, keepdims=True)
    scaled = (gate[:, :, None] * grad_out.astype(jnp.float32)[:, None, :]).astype(jnp.bfloat16)
    scaled = scaled.reshape(pair_count, model_width)
    flat_ids = expert_ids.reshape(-1)
    one_hot = (flat_ids[:, None] == jnp.arange(peers, dtype=jnp.int32)[None, :]).astype(
        jnp.bfloat16
    )
    pair_range = jnp.arange(pair_count, dtype=jnp.int32)
    lower = (pair_range[None, :] < pair_range[:, None]).astype(jnp.bfloat16)
    earlier = jnp.dot(lower, one_hot, preferred_element_type=jnp.float32)
    slot = jnp.sum(earlier * one_hot.astype(jnp.float32), axis=1).astype(jnp.int32)
    target = flat_ids * capacity + slot
    pair_of_slot = jnp.full((slot_count,), pair_count, jnp.int32).at[target].set(pair_range)
    token_of_slot = jnp.where(pair_of_slot < pair_count, pair_of_slot // top_count, tok_rows)
    zero_row = jnp.zeros((1, model_width), jnp.bfloat16)
    padded_tokens = jnp.concatenate([tokens, zero_row], axis=0)
    padded_scaled = jnp.concatenate([scaled, zero_row], axis=0)
    send_rows = padded_tokens[token_of_slot].reshape(peers, capacity, model_width)
    send_grads = padded_scaled[pair_of_slot].reshape(peers, capacity, model_width)
    gathered = (
        lax.all_gather(w_gate, "dp", axis=1, tiled=True),
        lax.all_gather(w_up, "dp", axis=1, tiled=True),
        lax.all_gather(w_down, "dp", axis=1, tiled=True),
    )
    gate_mat = gathered[0][0]
    up_mat = gathered[1][0]
    down_mat = gathered[2][0]
    arrived_rows, arrived_grads = (
        lax.all_to_all(send_rows, "expert", split_axis=0, concat_axis=0, tiled=True),
        lax.all_to_all(send_grads, "expert", split_axis=0, concat_axis=0, tiled=True),
    )
    rows_in = arrived_rows.reshape(slot_count, model_width)
    grads_in = arrived_grads.reshape(slot_count, model_width)
    grad_rows, grad_gate, grad_up, activation = backward_rows(
        rows_in, grads_in, gate_mat, up_mat, down_mat
    )
    returned = lax.all_to_all(
        grad_rows.reshape(peers, capacity, model_width),
        "expert",
        split_axis=0,
        concat_axis=0,
        tiled=True,
    )
    picked = returned.reshape(slot_count, model_width)[target].astype(jnp.float32)
    grad_tokens = jnp.sum(picked.reshape(tok_rows, top_count, model_width), axis=1).astype(
        jnp.bfloat16
    )
    quarter = model_width // data_groups
    term_gate = jnp.einsum(
        "rd,rf->df", rows_in, grad_gate, preferred_element_type=jnp.float32
    ).astype(jnp.bfloat16)
    term_up = jnp.einsum("rd,rf->df", rows_in, grad_up, preferred_element_type=jnp.float32).astype(
        jnp.bfloat16
    )
    term_down = jnp.einsum(
        "rd,rf->df", grads_in, activation, preferred_element_type=jnp.float32
    ).astype(jnp.bfloat16)
    stacked = jnp.stack([term_gate, term_up, term_down]).reshape(
        3, data_groups, quarter, hidden_width
    )
    arrived = lax.all_to_all(stacked, "dp", split_axis=1, concat_axis=1, tiled=True)
    summed = jnp.sum(arrived.astype(jnp.float32), axis=1).astype(jnp.bfloat16)
    return (grad_tokens, summed[0][None], summed[1][None], summed[2][None])


def contract_rows(lhs, rhs):
    return lax.dot_general(lhs, rhs, (((0,), (0,)), ((), ())), preferred_element_type=F32)


def layer_kernel(
    chips, tok_ref, grad_ref, ids_ref, numer_ref, wg_ref, wu_ref, wd_ref,
    out_tok, out_gate, out_up, out_down,
    xbuf, gbuf, nbuf, cbuf, sbuf, obuf, rbuf, wgu, wdn, acc_gu, acc_d, pbuf, qbuf, scaled, grads, acts,
    pre_buf, ga_buf, num_ref,
    w_send, w_recv, ring_send, ring_recv, sib_send, sib_recv,
    row_send, row_recv, sum_send, sum_recv, part_send, part_recv,
):
    half_ring = chips // 2
    group = lax.axis_index("dp")
    me = lax.axis_index("expert")
    core = lax.rem(me, 2)
    chip = lax.div(me, 2)
    lane = lax.rem(chip, 2)
    depth = lax.div(chip, 2)
    pos = jnp.where(lane == 0, depth, chips - 1 - depth)

    def device_at(ring_pos):
        far = ring_pos >= half_ring
        along = jnp.where(far, chips - 1 - ring_pos, ring_pos)
        return along * 4 + jnp.where(far, 2, 0) + core

    def ring(offset):
        return lax.rem(pos + offset + chips, chips)

    right = (group, device_at(ring(1)))
    left = (group, device_at(ring(-1)))
    sibling = (group, me + 1 - 2 * core)
    other = (1 - group, me)
    flows = (right, left)

    experts = 2 * chips
    expert_rows = lax.broadcasted_iota(jnp.int32, (experts, ids_ref.shape[1]), 0)
    by_expert = jnp.zeros(expert_rows.shape, jnp.int32)
    total = jnp.zeros(expert_rows.shape, jnp.int32)
    for k in range(ids_ref.shape[0]):
        numer = numer_ref[pl.ds(k, 1), :]
        by_expert = by_expert + jnp.where(ids_ref[pl.ds(k, 1), :] == expert_rows, numer, 0)
        total = total + numer
    num_ref[pl.ds(0, experts), :] = by_expert.astype(F32).astype(BF16)
    num_ref[pl.ds(experts, experts), :] = total.astype(F32).astype(BF16)

    barrier = pltpu.get_barrier_semaphore()
    for target in (right, left, sibling, other):
        pl.semaphore_signal(barrier, inc=1, device_id=target, device_id_type=MESH)
    pl.semaphore_wait(barrier, 4)

    started = []

    def copy(src, dst, send, recv, target):
        return pltpu.make_async_remote_copy(
            src_ref=src, dst_ref=dst, send_sem=send, recv_sem=recv,
            device_id=target, device_id_type=MESH,
        )

    def start(*args):
        op = copy(*args)
        op.start()
        started.append(op)

    share = wg_ref.shape[0]
    hidden = wg_ref.shape[1]
    block, width = tok_ref.shape
    own_at = pl.ds(pl.multiple_of(group * share, share), share)
    other_at = pl.ds(pl.multiple_of((1 - group) * share, share), share)

    def slot(f, d):
        return 0 if d == 0 else min(2 * d - 1 + f, chips - 1)

    own = (tok_ref, grad_ref, num_ref)
    bufs = (xbuf, gbuf, nbuf)

    def weight_places(rows):
        return (
            wgu.at[rows, pl.ds(0, hidden)],
            wgu.at[rows, pl.ds(hidden, hidden)],
            wdn.at[rows, :],
        )

    for a in (0, 2, 1):
        for f in range(2):
            start(own[a], bufs[a].at[slot(f, 1), core], ring_send.at[a, f, 0], ring_recv.at[a, f, 0], flows[f])
    for k, ref in enumerate((wg_ref, wu_ref, wd_ref)):
        start(ref, weight_places(own_at)[k], w_send.at[k], w_recv.at[k], other)
    for a in (0, 2, 1):
        start(own[a], bufs[a].at[0, core], sib_send.at[a, 0], sib_recv.at[a, 0], sibling)
    for a in range(3):
        bufs[a][0, core] = own[a][...]
    wgu[own_at, pl.ds(0, hidden)] = wg_ref[...]
    wgu[own_at, pl.ds(hidden, hidden)] = wu_ref[...]
    wdn[own_at, :] = wd_ref[...]

    def part(a, s, c, step, f):
        if step == half_ring:
            n = bufs[a].shape[2] // 2
            return bufs[a].at[s, c, pl.ds(f * n, n)]
        return bufs[a].at[s, c]

    def arrive(a, step):
        for f in range(2):
            ref = part(a, slot(f, step), core, step, f)
            copy(ref, ref, ring_send.at[a, f, step - 1], ring_recv.at[a, f, step - 1], flows[f]).wait_recv()
            if step < half_ring:
                src = part(a, slot(f, step), core, step + 1, f)
                dst = part(a, slot(f, step + 1), core, step + 1, f)
                start(src, dst, ring_send.at[a, f, step], ring_recv.at[a, f, step], flows[f])
            k = 2 * step - 1 + f
            start(ref, ref, sib_send.at[a, k], sib_recv.at[a, k], sibling)

    def arrive_sibling(step, arrays=(0, 1, 2)):
        for a in arrays:
            for f in range(2 if step else 1):
                ref = part(a, slot(f, step), 1 - core, step, f)
                k = 2 * step - 1 + f if step else 0
                copy(ref, ref, sib_send.at[a, k], sib_recv.at[a, k], sibling).wait_recv()

    per_slot = 2 * block
    row_ids = lax.broadcasted_iota(jnp.int32, (2 * experts, 256), 0)
    col_ids = lax.broadcasted_iota(jnp.int32, (2 * experts, 256), 1)
    wanted = jnp.where(col_ids < 128, me, experts)
    select = jnp.where(row_ids == wanted, 1.0, 0.0).astype(BF16)

    def span(slots):
        return pl.ds(slots[0] * per_slot, len(slots) * per_slot)

    def tokens_of(slots, cols=slice(None)):
        return xbuf[slots[0] : slots[-1] + 1, :, :, cols].reshape(len(slots) * per_slot, -1)

    def scale(slots):
        for s in slots:
            for b in range(2):
                both = contract_rows(nbuf[s, b], select)
                gate = both[:, :128] / both[:, 128:]
                for k in range(width // 128):
                    cols = pl.ds(k * 128, 128)
                    scaled[pl.ds(s * per_slot + b * block, block), cols] = (
                        gate * gbuf[s, b, :, cols].astype(F32)
                    ).astype(BF16)

    def pre_part(slots, at):
        x = tokens_of(slots, at)
        return jnp.dot(x, wgu[at, :], preferred_element_type=F32)

    def ga_part(slots, at):
        return jnp.dot(scaled[span(slots), at], wdn[at, :], preferred_element_type=F32)

    def pointwise(slots, pre, grad_act):
        where = span(slots)
        pre_gate = pre[:, :hidden]
        pre_up = pre[:, hidden:]
        sig = jax.nn.sigmoid(pre_gate)
        silu = pre_gate * sig
        acts[where, :] = (silu * pre_up).astype(BF16)
        grads[where, pl.ds(hidden, hidden)] = (grad_act * silu).astype(BF16)
        grads[where, pl.ds(0, hidden)] = (
            grad_act * pre_up * sig * (1.0 + pre_gate * (1.0 - sig))
        ).astype(BF16)

    def back(slots):
        rows = lax.dot_general(
            grads[span(slots), :], wgu[...], (((1,), (1,)), ((), ())), preferred_element_type=F32
        )
        cbuf[slots[0] : slots[-1] + 1] = rows.astype(BF16).reshape(len(slots), 2, block, width)
        for s in slots:
            start(cbuf.at[s, 1 - core], sbuf.at[s], row_send.at[s], row_recv.at[s], sibling)

    def terms(slots, at, k):
        where = span(slots)
        if k == 2:
            return contract_rows(scaled[where, at], acts[where, :])
        return contract_rows(tokens_of(slots, at), grads[where, pl.ds(k * hidden, hidden)])

    def wait_weight(k):
        ref = weight_places(other_at)[k]
        copy(ref, ref, w_send.at[k], w_recv.at[k], other).wait_recv()

    slots_a, slots_b, slots_c, slots_d, slots_e = [0], [1, 2], [3, 4], [5, 6], [7]
    everything = slice(None)

    def point(slots):
        pointwise(slots, pre_buf[span(slots), :], ga_buf[span(slots), :])

    arrive_sibling(0)
    scale(slots_a)
    pre_buf[span(slots_a), :] = pre_part(slots_a, own_at)
    ga_buf[span(slots_a), :] = ga_part(slots_a, own_at)
    arrive(0, 1)
    arrive_sibling(1, (0,))
    pre_buf[span(slots_b), :] = pre_part(slots_b, own_at)
    arrive(2, 1)
    arrive(1, 1)
    arrive_sibling(1, (1, 2))
    scale(slots_b)
    ga_buf[span(slots_b), :] = ga_part(slots_b, own_at)
    arrive(0, 2)
    arrive_sibling(2, (0,))
    wait_weight(0)
    wait_weight(1)
    pre_buf[span(slots_a), :] += pre_part(slots_a, other_at)
    pre_buf[span(slots_b), :] += pre_part(slots_b, other_at)
    arrive(2, 2)
    arrive(1, 2)
    pre_buf[span(slots_c), :] = pre_part(slots_c, everything)
    arrive_sibling(2, (1, 2))
    scale(slots_c)
    wait_weight(2)
    ga_buf[span(slots_a), :] += ga_part(slots_a, other_at)
    point(slots_a)
    ga_buf[span(slots_b), :] += ga_part(slots_b, other_at)
    point(slots_b)
    arrive(0, 3)
    ga_buf[span(slots_c), :] = ga_part(slots_c, everything)
    point(slots_c)
    arrive_sibling(3, (0,))
    pre_buf[span(slots_d), :] = pre_part(slots_d, everything)
    arrive(2, 3)
    arrive(1, 3)
    slots_abc = slots_a + slots_b + slots_c
    for k in range(2):
        acc_gu[:, pl.ds(k * hidden, hidden)] = terms(slots_abc, other_at, k)
    acc_d[...] = terms(slots_abc, other_at, 2)
    arrive_sibling(3, (1, 2))
    scale(slots_d)
    ga_buf[span(slots_d), :] = ga_part(slots_d, everything)
    point(slots_d)
    arrive(0, 4)
    arrive(2, 4)
    back(slots_d)
    arrive_sibling(4, (0, 2))
    pre_e = pre_part(slots_e, everything)
    pre_buf[span(slots_e), :] = pre_e
    arrive(1, 4)
    arrive_sibling(4, (1,))
    scale(slots_e)
    ga_buf[span(slots_e), :] = ga_part(slots_e, everything)
    point(slots_e)

    slots_de = slots_d + slots_e

    def send_term(k):
        held = acc_d[...] if k == 2 else acc_gu[:, pl.ds(k * hidden, hidden)]
        pbuf[k] = (held + terms(slots_de, other_at, k)).astype(BF16)
        start(pbuf.at[k], qbuf.at[k], part_send.at[k], part_recv.at[k], other)

    send_term(0)
    back(slots_e)
    send_term(1)

    half = block // 2
    got_rows = set()

    def row_sum(s, h):
        if s not in got_rows:
            got_rows.add(s)
            copy(sbuf.at[s], sbuf.at[s], row_send.at[s], row_recv.at[s], sibling).wait_recv()
        at = pl.ds(h * half, half)
        return cbuf[s, core, at].astype(F32) + sbuf[s, at].astype(F32)

    def order(f):
        listed = [(half_ring, f)]
        for d in range(half_ring - 1, 0, -1):
            listed += [(d, 1 - f), (d, f)]
        return listed

    def incoming(f, d, h):
        j = order(f).index((d + 1, h))
        ref = rbuf.at[f, j]
        copy(ref, ref, sum_send.at[f, j], sum_recv.at[f, j], flows[f]).wait_recv()
        return rbuf[f, j].astype(F32)

    outs = (out_gate, out_up, out_down)

    def own_term(k):
        outs[k][...] = terms(list(range(chips)), own_at, k).astype(BF16)

    between = {
        1: lambda: (send_term(2), back(slots_c)),
        2: lambda: back(slots_b),
        3: lambda: back(slots_a),
        4: lambda: own_term(0),
        5: lambda: own_term(1),
        6: lambda: own_term(2),
    }

    for j in range(len(order(0))):
        for f in range(2):
            d, h = order(f)[j]
            value = row_sum(slot(1 - f, d), h)
            if (d + 1, h) in order(f):
                value = value + incoming(f, d, h)
            obuf[f, j] = value.astype(BF16)
            start(obuf.at[f, j], rbuf.at[f, j], sum_send.at[f, j], sum_recv.at[f, j], flows[f])
        if j in between:
            between[j]()
    for h in range(2):
        value = row_sum(0, h) + incoming(0, 0, h) + incoming(1, 0, h)
        out_tok[pl.ds(h * half, half), :] = value.astype(BF16)

    for k, out in enumerate(outs):
        copy(qbuf.at[k], qbuf.at[k], part_send.at[k], part_recv.at[k], other).wait_recv()
        out[...] = (out[...].astype(F32) + qbuf[k].astype(F32)).astype(BF16)
    for op in started:
        op.wait_send()


def write_out(*refs):
    sems = refs[-1]
    copies = [pltpu.make_async_copy(refs[k], refs[4 + k], sems.at[k]) for k in range(4)]
    for op in copies:
        op.start()
    for op in copies:
        op.wait()


def on_device_dense(tokens, grad_out, expert_ids, gate_numer, w_gate, w_up, w_down):
    peers = lax.axis_size("expert")
    chips = peers // 2
    block, width = tokens.shape
    share, hidden = w_gate.shape[1:]
    depth = share * lax.axis_size("dp")
    messages = chips - 1
    rows = peers * block
    early = rows
    dma = pltpu.SemaphoreType.DMA
    vmem = pl.BlockSpec(memory_space=pltpu.VMEM)
    outs = pl.pallas_call(
        functools.partial(layer_kernel, chips),
        out_shape=(jax.ShapeDtypeStruct((block, width), BF16),)
        + (jax.ShapeDtypeStruct((share, hidden), BF16),) * 3,
        in_specs=[vmem] * 7,
        out_specs=(vmem,) * 4,
        scratch_shapes=[
            pltpu.VMEM((chips, 2, block, width), BF16),
            pltpu.VMEM((chips, 2, block, width), BF16),
            pltpu.VMEM((chips, 2, 2 * peers, block), BF16),
            pltpu.VMEM((chips, 2, block, width), BF16),
            pltpu.VMEM((chips, block, width), BF16),
            pltpu.VMEM((2, messages, block // 2, width), BF16),
            pltpu.VMEM((2, messages, block // 2, width), BF16),
            pltpu.VMEM((depth, 2 * hidden), BF16),
            pltpu.VMEM((depth, hidden), BF16),
            pltpu.VMEM((share, 2 * hidden), F32),
            pltpu.VMEM((share, hidden), F32),
            pltpu.VMEM((3, share, hidden), BF16),
            pltpu.VMEM((3, share, hidden), BF16),
            pltpu.VMEM((rows, width), BF16),
            pltpu.VMEM((rows, 2 * hidden), BF16),
            pltpu.VMEM((rows, hidden), BF16),
            pltpu.VMEM((early, 2 * hidden), F32),
            pltpu.VMEM((early, hidden), F32),
            pltpu.VMEM((2 * peers, block), BF16),
            dma((3,)), dma((3,)),
            dma((3, 2, chips // 2)), dma((3, 2, chips // 2)),
            dma((3, chips + 1)), dma((3, chips + 1)),
            dma((chips,)), dma((chips,)),
            dma((2, messages)), dma((2, messages)),
            dma((3,)), dma((3,)),
        ],
        compiler_params=pltpu.CompilerParams(
            collective_id=0, has_side_effects=True, vmem_limit_bytes=58 * 1024 * 1024
        ),
        cost_estimate=pl.CostEstimate(
            flops=16 * peers * block * width * hidden, bytes_accessed=8 * block * width, transcendentals=0
        ),
    )(tokens, grad_out, expert_ids.T, gate_numer.T, w_gate[0], w_up[0], w_down[0])
    outs = pl.pallas_call(
        write_out,
        out_shape=tuple(jax.ShapeDtypeStruct(value.shape, value.dtype) for value in outs),
        in_specs=[pl.BlockSpec(memory_space=pltpu.HBM)] * 4,
        out_specs=(pl.BlockSpec(memory_space=pltpu.HBM),) * 4,
        scratch_shapes=[dma((4,))],
    )(*outs)
    return (outs[0],) + tuple(value[None] for value in outs[1:])


def solution(mesh):
    return jax.shard_map(
        on_device_dense if mesh.shape["expert"] == 16 else on_device_routed,
        mesh=mesh,
        in_specs=(
            P(("dp", "expert"), None),
            P(("dp", "expert"), None),
            P(("dp", "expert"), None),
            P(("dp", "expert"), None),
            P("expert", "dp", None),
            P("expert", "dp", None),
            P("expert", "dp", None),
        ),
        out_specs=(
            P(("dp", "expert"), None),
            P("expert", "dp", None),
            P("expert", "dp", None),
            P("expert", "dp", None),
        ),
        check_vma=False,
    )
```

```python
import functools

import jax
import jax.numpy as jnp
from jax import lax
from jax.experimental import pallas as pl
from jax.experimental.pallas import tpu as pltpu
from jax.sharding import PartitionSpec as P

MESH = pl.DeviceIdType.MESH
F32 = jnp.float32
BF16 = jnp.bfloat16


def backward_rows(rows_in, grads_in, gate_mat, up_mat, down_mat):
    pre_gate = jnp.dot(rows_in, gate_mat, preferred_element_type=jnp.float32)
    pre_up = jnp.dot(rows_in, up_mat, preferred_element_type=jnp.float32)
    sigmoid_gate = jax.nn.sigmoid(pre_gate)
    activation = (pre_gate * sigmoid_gate * pre_up).astype(jnp.bfloat16)
    grad_act = jnp.dot(grads_in, down_mat, preferred_element_type=jnp.float32)
    grad_up = (grad_act * pre_gate * sigmoid_gate).astype(jnp.bfloat16)
    grad_gate = (grad_act * pre_up * sigmoid_gate * (1.0 + pre_gate * (1.0 - sigmoid_gate))).astype(
        jnp.bfloat16
    )
    grad_rows = jnp.einsum("rf,df->rd", grad_gate, gate_mat, preferred_element_type=jnp.float32)
    grad_rows = grad_rows + jnp.einsum(
        "rf,df->rd", grad_up, up_mat, preferred_element_type=jnp.float32
    )
    return (grad_rows.astype(jnp.bfloat16), grad_gate, grad_up, activation)


def on_device_routed(tokens, grad_out, expert_ids, gate_numer, w_gate, w_up, w_down):
    peers = lax.axis_size("expert")
    data_groups = lax.axis_size("dp")
    tok_rows = tokens.shape[0]
    model_width = tokens.shape[1]
    top_count = expert_ids.shape[1]
    hidden_width = w_gate.shape[2]
    mean_rows = tok_rows * top_count // peers
    capacity = min(tok_rows, mean_rows + tok_rows * top_count // (8 * peers))
    pair_count = tok_rows * top_count
    slot_count = peers * capacity
    numer = gate_numer.astype(jnp.float32)
    gate = numer / jnp.sum(numer, axis=1, keepdims=True)
    scaled = (gate[:, :, None] * grad_out.astype(jnp.float32)[:, None, :]).astype(jnp.bfloat16)
    scaled = scaled.reshape(pair_count, model_width)
    flat_ids = expert_ids.reshape(-1)
    one_hot = (flat_ids[:, None] == jnp.arange(peers, dtype=jnp.int32)[None, :]).astype(
        jnp.bfloat16
    )
    pair_range = jnp.arange(pair_count, dtype=jnp.int32)
    lower = (pair_range[None, :] < pair_range[:, None]).astype(jnp.bfloat16)
    earlier = jnp.dot(lower, one_hot, preferred_element_type=jnp.float32)
    slot = jnp.sum(earlier * one_hot.astype(jnp.float32), axis=1).astype(jnp.int32)
    target = flat_ids * capacity + slot
    pair_of_slot = jnp.full((slot_count,), pair_count, jnp.int32).at[target].set(pair_range)
    token_of_slot = jnp.where(pair_of_slot < pair_count, pair_of_slot // top_count, tok_rows)
    zero_row = jnp.zeros((1, model_width), jnp.bfloat16)
    padded_tokens = jnp.concatenate([tokens, zero_row], axis=0)
    padded_scaled = jnp.concatenate([scaled, zero_row], axis=0)
    send_rows = padded_tokens[token_of_slot].reshape(peers, capacity, model_width)
    send_grads = padded_scaled[pair_of_slot].reshape(peers, capacity, model_width)
    gathered = (
        lax.all_gather(w_gate, "dp", axis=1, tiled=True),
        lax.all_gather(w_up, "dp", axis=1, tiled=True),
        lax.all_gather(w_down, "dp", axis=1, tiled=True),
    )
    gate_mat = gathered[0][0]
    up_mat = gathered[1][0]
    down_mat = gathered[2][0]
    arrived_rows, arrived_grads = (
        lax.all_to_all(send_rows, "expert", split_axis=0, concat_axis=0, tiled=True),
        lax.all_to_all(send_grads, "expert", split_axis=0, concat_axis=0, tiled=True),
    )
    rows_in = arrived_rows.reshape(slot_count, model_width)
    grads_in = arrived_grads.reshape(slot_count, model_width)
    grad_rows, grad_gate, grad_up, activation = backward_rows(
        rows_in, grads_in, gate_mat, up_mat, down_mat
    )
    returned = lax.all_to_all(
        grad_rows.reshape(peers, capacity, model_width),
        "expert",
        split_axis=0,
        concat_axis=0,
        tiled=True,
    )
    picked = returned.reshape(slot_count, model_width)[target].astype(jnp.float32)
    grad_tokens = jnp.sum(picked.reshape(tok_rows, top_count, model_width), axis=1).astype(
        jnp.bfloat16
    )
    quarter = model_width // data_groups
    term_gate = jnp.einsum(
        "rd,rf->df", rows_in, grad_gate, preferred_element_type=jnp.float32
    ).astype(jnp.bfloat16)
    term_up = jnp.einsum("rd,rf->df", rows_in, grad_up, preferred_element_type=jnp.float32).astype(
        jnp.bfloat16
    )
    term_down = jnp.einsum(
        "rd,rf->df", grads_in, activation, preferred_element_type=jnp.float32
    ).astype(jnp.bfloat16)
    stacked = jnp.stack([term_gate, term_up, term_down]).reshape(
        3, data_groups, quarter, hidden_width
    )
    arrived = lax.all_to_all(stacked, "dp", split_axis=1, concat_axis=1, tiled=True)
    summed = jnp.sum(arrived.astype(jnp.float32), axis=1).astype(jnp.bfloat16)
    return (grad_tokens, summed[0][None], summed[1][None], summed[2][None])


def contract_rows(lhs, rhs):
    return lax.dot_general(lhs, rhs, (((0,), (0,)), ((), ())), preferred_element_type=F32)


def layer_kernel(
    chips, tok_ref, grad_ref, ids_ref, numer_ref, wg_ref, wu_ref, wd_ref,
    out_tok, out_gate, out_up, out_down,
    xbuf, gbuf, nbuf, cbuf, sbuf, obuf, rbuf, wgu, wdn, acc_gu, acc_d, pbuf, qbuf, scaled, grads, acts,
    pre_buf, ga_buf, num_ref,
    w_send, w_recv, ring_send, ring_recv, sib_send, sib_recv,
    row_send, row_recv, sum_send, sum_recv, part_send, part_recv,
):
    half_ring = chips // 2
    group = lax.axis_index("dp")
    me = lax.axis_index("expert")
    core = lax.rem(me, 2)
    chip = lax.div(me, 2)
    lane = lax.rem(chip, 2)
    depth = lax.div(chip, 2)
    pos = jnp.where(lane == 0, depth, chips - 1 - depth)

    def device_at(ring_pos):
        far = ring_pos >= half_ring
        along = jnp.where(far, chips - 1 - ring_pos, ring_pos)
        return along * 4 + jnp.where(far, 2, 0) + core

    def ring(offset):
        return lax.rem(pos + offset + chips, chips)

    right = (group, device_at(ring(1)))
    left = (group, device_at(ring(-1)))
    sibling = (group, me + 1 - 2 * core)
    other = (1 - group, me)
    flows = (right, left)

    experts = 2 * chips
    expert_rows = lax.broadcasted_iota(jnp.int32, (experts, ids_ref.shape[1]), 0)
    by_expert = jnp.zeros(expert_rows.shape, jnp.int32)
    total = jnp.zeros(expert_rows.shape, jnp.int32)
    for k in range(ids_ref.shape[0]):
        numer = numer_ref[pl.ds(k, 1), :]
        by_expert = by_expert + jnp.where(ids_ref[pl.ds(k, 1), :] == expert_rows, numer, 0)
        total = total + numer
    num_ref[pl.ds(0, experts), :] = by_expert.astype(F32).astype(BF16)
    num_ref[pl.ds(experts, experts), :] = total.astype(F32).astype(BF16)

    barrier = pltpu.get_barrier_semaphore()
    for target in (right, left, sibling, other):
        pl.semaphore_signal(barrier, inc=1, device_id=target, device_id_type=MESH)
    pl.semaphore_wait(barrier, 4)

    started = []

    def copy(src, dst, send, recv, target):
        return pltpu.make_async_remote_copy(
            src_ref=src, dst_ref=dst, send_sem=send, recv_sem=recv,
            device_id=target, device_id_type=MESH,
        )

    def start(*args):
        op = copy(*args)
        op.start()
        started.append(op)

    share = wg_ref.shape[0]
    hidden = wg_ref.shape[1]
    block, width = tok_ref.shape
    own_at = pl.ds(pl.multiple_of(group * share, share), share)
    other_at = pl.ds(pl.multiple_of((1 - group) * share, share), share)

    def slot(f, d):
        return 0 if d == 0 else min(2 * d - 1 + f, chips - 1)

    quarter = width // 4
    bufs = (xbuf, gbuf, nbuf, xbuf)
    columns = (pl.ds(0, quarter), pl.ds(0, width), pl.ds(0, num_ref.shape[1]), pl.ds(quarter, width - quarter))
    own = (tok_ref.at[:, columns[0]], grad_ref, num_ref, tok_ref.at[:, columns[3]])

    def weight_places(rows):
        return (
            wgu.at[rows, pl.ds(0, hidden)],
            wgu.at[rows, pl.ds(hidden, hidden)],
            wdn.at[rows, :],
        )

    for a in (0, 3, 2, 1):
        for f in range(2):
            start(own[a], bufs[a].at[slot(f, 1), core, :, columns[a]], ring_send.at[a, f, 0], ring_recv.at[a, f, 0], flows[f])
    for k, ref in enumerate((wg_ref, wu_ref, wd_ref)):
        start(ref, weight_places(own_at)[k], w_send.at[k], w_recv.at[k], other)
    for a in (0, 3, 2, 1):
        start(own[a], bufs[a].at[0, core, :, columns[a]], sib_send.at[a, 0], sib_recv.at[a, 0], sibling)
    for buf, ref in ((xbuf, tok_ref), (gbuf, grad_ref), (nbuf, num_ref)):
        buf[0, core] = ref[...]
    wgu[own_at, pl.ds(0, hidden)] = wg_ref[...]
    wgu[own_at, pl.ds(hidden, hidden)] = wu_ref[...]
    wdn[own_at, :] = wd_ref[...]

    def part(a, s, c, step, f):
        if step == half_ring:
            n = bufs[a].shape[2] // 2
            return bufs[a].at[s, c, pl.ds(f * n, n), columns[a]]
        return bufs[a].at[s, c, :, columns[a]]

    def arrive(a, step):
        for f in range(2):
            ref = part(a, slot(f, step), core, step, f)
            copy(ref, ref, ring_send.at[a, f, step - 1], ring_recv.at[a, f, step - 1], flows[f]).wait_recv()
            if step < half_ring:
                src = part(a, slot(f, step), core, step + 1, f)
                dst = part(a, slot(f, step + 1), core, step + 1, f)
                start(src, dst, ring_send.at[a, f, step], ring_recv.at[a, f, step], flows[f])
            k = 2 * step - 1 + f
            start(ref, ref, sib_send.at[a, k], sib_recv.at[a, k], sibling)

    def arrive_sibling(step, arrays=(0, 3, 2, 1)):
        for a in arrays:
            for f in range(2 if step else 1):
                ref = part(a, slot(f, step), 1 - core, step, f)
                k = 2 * step - 1 + f if step else 0
                copy(ref, ref, sib_send.at[a, k], sib_recv.at[a, k], sibling).wait_recv()

    per_slot = 2 * block
    row_ids = lax.broadcasted_iota(jnp.int32, (2 * experts, 256), 0)
    col_ids = lax.broadcasted_iota(jnp.int32, (2 * experts, 256), 1)
    wanted = jnp.where(col_ids < 128, me, experts)
    select = jnp.where(row_ids == wanted, 1.0, 0.0).astype(BF16)

    def span(slots):
        return pl.ds(slots[0] * per_slot, len(slots) * per_slot)

    def tokens_of(slots, cols=slice(None)):
        return xbuf[slots[0] : slots[-1] + 1, :, :, cols].reshape(len(slots) * per_slot, -1)

    def scale(slots):
        for s in slots:
            for b in range(2):
                both = contract_rows(nbuf[s, b], select)
                gate = both[:, :128] / both[:, 128:]
                for k in range(width // 128):
                    cols = pl.ds(k * 128, 128)
                    scaled[pl.ds(s * per_slot + b * block, block), cols] = (
                        gate * gbuf[s, b, :, cols].astype(F32)
                    ).astype(BF16)

    def pre_part(slots, at):
        x = tokens_of(slots, at)
        return jnp.dot(x, wgu[at, :], preferred_element_type=F32)

    def ga_part(slots, at):
        return jnp.dot(scaled[span(slots), at], wdn[at, :], preferred_element_type=F32)

    def pointwise(slots, pre, grad_act):
        where = span(slots)
        pre_gate = pre[:, :hidden]
        pre_up = pre[:, hidden:]
        sig = jax.nn.sigmoid(pre_gate)
        silu = pre_gate * sig
        acts[where, :] = (silu * pre_up).astype(BF16)
        grads[where, pl.ds(hidden, hidden)] = (grad_act * silu).astype(BF16)
        grads[where, pl.ds(0, hidden)] = (
            grad_act * pre_up * sig * (1.0 + pre_gate * (1.0 - sig))
        ).astype(BF16)

    def back(slots):
        rows = lax.dot_general(
            grads[span(slots), :], wgu[...], (((1,), (1,)), ((), ())), preferred_element_type=F32
        )
        cbuf[slots[0] : slots[-1] + 1] = rows.astype(BF16).reshape(len(slots), 2, block, width)
        for s in slots:
            start(cbuf.at[s, 1 - core], sbuf.at[s], row_send.at[s], row_recv.at[s], sibling)

    def terms(slots, at, k):
        where = span(slots)
        if k == 2:
            return contract_rows(scaled[where, at], acts[where, :])
        return contract_rows(tokens_of(slots, at), grads[where, pl.ds(k * hidden, hidden)])

    def wait_weight(k):
        ref = weight_places(other_at)[k]
        copy(ref, ref, w_send.at[k], w_recv.at[k], other).wait_recv()

    half = block // 2
    got_rows = set()

    def row_sum(s, h):
        if s not in got_rows:
            got_rows.add(s)
            copy(sbuf.at[s], sbuf.at[s], row_send.at[s], row_recv.at[s], sibling).wait_recv()
        at = pl.ds(h * half, half)
        return cbuf[s, core, at].astype(F32) + sbuf[s, at].astype(F32)

    def order(f):
        listed = [(half_ring - 1, 1 - f), (half_ring, f), (half_ring - 1, f)]
        for d in range(half_ring - 2, 0, -1):
            listed += [(d, 1 - f), (d, f)]
        return listed

    def incoming(f, d, h):
        j = order(f).index((d + 1, h))
        ref = rbuf.at[f, j]
        copy(ref, ref, sum_send.at[f, j], sum_recv.at[f, j], flows[f]).wait_recv()
        return rbuf[f, j].astype(F32)

    def send_sums(j):
        for f in range(2):
            d, h = order(f)[j]
            value = row_sum(slot(1 - f, d), h)
            if (d + 1, h) in order(f):
                value = value + incoming(f, d, h)
            obuf[f, j] = value.astype(BF16)
            start(obuf.at[f, j], rbuf.at[f, j], sum_send.at[f, j], sum_recv.at[f, j], flows[f])

    slots_a, slots_b, slots_c, slots_d, slots_e = [0], [1, 2], [3, 4], [5, 6], [7]
    everything = slice(None)

    def point(slots):
        pointwise(slots, pre_buf[span(slots), :], ga_buf[span(slots), :])

    arrive_sibling(0)
    scale(slots_a)
    pre_buf[span(slots_a), :] = pre_part(slots_a, own_at)
    ga_buf[span(slots_a), :] = ga_part(slots_a, own_at)
    arrive(0, 1)
    arrive(3, 1)
    arrive_sibling(1, (0, 3))
    pre_buf[span(slots_b), :] = pre_part(slots_b, own_at)
    arrive(2, 1)
    arrive(1, 1)
    arrive_sibling(1, (1, 2))
    scale(slots_b)
    ga_buf[span(slots_b), :] = ga_part(slots_b, own_at)
    arrive(0, 2)
    arrive(3, 2)
    arrive_sibling(2, (0, 3))
    wait_weight(0)
    wait_weight(1)
    pre_buf[span(slots_a), :] += pre_part(slots_a, other_at)
    pre_buf[span(slots_b), :] += pre_part(slots_b, other_at)
    arrive(2, 2)
    arrive(1, 2)
    pre_buf[span(slots_c), :] = pre_part(slots_c, everything)
    arrive_sibling(2, (1, 2))
    scale(slots_c)
    wait_weight(2)
    ga_buf[span(slots_a), :] += ga_part(slots_a, other_at)
    point(slots_a)
    ga_buf[span(slots_b), :] += ga_part(slots_b, other_at)
    point(slots_b)
    arrive(0, 3)
    arrive(3, 3)
    ga_buf[span(slots_c), :] = ga_part(slots_c, everything)
    point(slots_c)
    arrive_sibling(3, (0, 3))
    pre_buf[span(slots_d), :] = pre_part(slots_d, everything)
    arrive(2, 3)
    arrive(1, 3)
    slots_abc = slots_a + slots_b + slots_c
    for k in range(2):
        acc_gu[:, pl.ds(k * hidden, hidden)] = terms(slots_abc, other_at, k)
    acc_d[...] = terms(slots_abc, other_at, 2)
    arrive_sibling(3, (1, 2))
    scale(slots_d)
    ga_buf[span(slots_d), :] = ga_part(slots_d, everything)
    point(slots_d)
    arrive(0, 4)
    arrive(3, 4)
    arrive(2, 4)
    back(slots_d)
    arrive_sibling(4, (0, 3, 2))
    pre_e = pre_part(slots_e, everything)
    pre_buf[span(slots_e), :] = pre_e
    for k in range(2):
        acc_gu[:, pl.ds(k * hidden, hidden)] += terms(slots_d, other_at, k)
    acc_d[...] += terms(slots_d, other_at, 2)
    send_sums(0)
    arrive(1, 4)
    arrive_sibling(4, (1,))
    scale(slots_e)
    ga_buf[span(slots_e), :] = ga_part(slots_e, everything)
    point(slots_e)

    def send_term(k):
        held = acc_d[...] if k == 2 else acc_gu[:, pl.ds(k * hidden, hidden)]
        pbuf[k] = (held + terms(slots_e, other_at, k)).astype(BF16)
        start(pbuf.at[k], qbuf.at[k], part_send.at[k], part_recv.at[k], other)

    send_term(0)
    back(slots_e)
    send_term(1)

    outs = (out_gate, out_up, out_down)

    def own_term(k):
        outs[k][...] = terms(list(range(chips)), own_at, k).astype(BF16)

    between = {
        1: lambda: (send_term(2), back(slots_c)),
        2: lambda: back(slots_b),
        3: lambda: back(slots_a),
        4: lambda: own_term(0),
        5: lambda: own_term(1),
        6: lambda: own_term(2),
    }

    for j in range(1, len(order(0))):
        send_sums(j)
        if j in between:
            between[j]()
    for h in range(2):
        value = row_sum(0, h) + incoming(0, 0, h) + incoming(1, 0, h)
        out_tok[pl.ds(h * half, half), :] = value.astype(BF16)

    for k, out in enumerate(outs):
        copy(qbuf.at[k], qbuf.at[k], part_send.at[k], part_recv.at[k], other).wait_recv()
        out[...] = (out[...].astype(F32) + qbuf[k].astype(F32)).astype(BF16)
    for op in started:
        op.wait_send()


def write_out(*refs):
    ins, outs, held, sems = refs[:4], refs[4:8], refs[8:12], refs[12]
    reads = [pltpu.make_async_copy(ins[k], held[k], sems.at[k]) for k in range(4)]
    writes = [pltpu.make_async_copy(held[k], outs[k], sems.at[4 + k]) for k in range(4)]
    for op in reads:
        op.start()
    for k in range(4):
        reads[k].wait()
        writes[k].start()
    for op in writes:
        op.wait()


def on_device_dense(tokens, grad_out, expert_ids, gate_numer, w_gate, w_up, w_down):
    peers = lax.axis_size("expert")
    chips = peers // 2
    block, width = tokens.shape
    share, hidden = w_gate.shape[1:]
    depth = share * lax.axis_size("dp")
    messages = chips - 1
    rows = peers * block
    early = rows
    dma = pltpu.SemaphoreType.DMA
    vmem = pl.BlockSpec(memory_space=pltpu.VMEM)
    outs = pl.pallas_call(
        functools.partial(layer_kernel, chips),
        out_shape=(jax.ShapeDtypeStruct((block, width), BF16),)
        + (jax.ShapeDtypeStruct((share, hidden), BF16),) * 3,
        in_specs=[vmem] * 7,
        out_specs=(vmem,) * 4,
        scratch_shapes=[
            pltpu.VMEM((chips, 2, block, width), BF16),
            pltpu.VMEM((chips, 2, block, width), BF16),
            pltpu.VMEM((chips, 2, 2 * peers, block), BF16),
            pltpu.VMEM((chips, 2, block, width), BF16),
            pltpu.VMEM((chips, block, width), BF16),
            pltpu.VMEM((2, messages, block // 2, width), BF16),
            pltpu.VMEM((2, messages, block // 2, width), BF16),
            pltpu.VMEM((depth, 2 * hidden), BF16),
            pltpu.VMEM((depth, hidden), BF16),
            pltpu.VMEM((share, 2 * hidden), F32),
            pltpu.VMEM((share, hidden), F32),
            pltpu.VMEM((3, share, hidden), BF16),
            pltpu.VMEM((3, share, hidden), BF16),
            pltpu.VMEM((rows, width), BF16),
            pltpu.VMEM((rows, 2 * hidden), BF16),
            pltpu.VMEM((rows, hidden), BF16),
            pltpu.VMEM((early, 2 * hidden), F32),
            pltpu.VMEM((early, hidden), F32),
            pltpu.VMEM((2 * peers, block), BF16),
            dma((3,)), dma((3,)),
            dma((4, 2, chips // 2)), dma((4, 2, chips // 2)),
            dma((4, chips + 1)), dma((4, chips + 1)),
            dma((chips,)), dma((chips,)),
            dma((2, messages)), dma((2, messages)),
            dma((3,)), dma((3,)),
        ],
        compiler_params=pltpu.CompilerParams(
            collective_id=0, has_side_effects=True, vmem_limit_bytes=58 * 1024 * 1024
        ),
        cost_estimate=pl.CostEstimate(
            flops=16 * peers * block * width * hidden, bytes_accessed=8 * block * width, transcendentals=0
        ),
    )(tokens, grad_out, expert_ids.T, gate_numer.T, w_gate[0], w_up[0], w_down[0])
    outs = pl.pallas_call(
        write_out,
        out_shape=tuple(jax.ShapeDtypeStruct(value.shape, value.dtype) for value in outs),
        in_specs=[pl.BlockSpec(memory_space=pltpu.HBM)] * 4,
        out_specs=(pl.BlockSpec(memory_space=pltpu.HBM),) * 4,
        scratch_shapes=[pltpu.VMEM(value.shape, value.dtype) for value in outs] + [dma((8,))],
    )(*outs)
    return (outs[0],) + tuple(value[None] for value in outs[1:])


def solution(mesh):
    return jax.shard_map(
        on_device_dense if mesh.shape["expert"] == 16 else on_device_routed,
        mesh=mesh,
        in_specs=(
            P(("dp", "expert"), None),
            P(("dp", "expert"), None),
            P(("dp", "expert"), None),
            P(("dp", "expert"), None),
            P("expert", "dp", None),
            P("expert", "dp", None),
            P("expert", "dp", None),
        ),
        out_specs=(
            P(("dp", "expert"), None),
            P("expert", "dp", None),
            P("expert", "dp", None),
            P("expert", "dp", None),
        ),
        check_vma=False,
    )
```

```python
import functools

import jax
import jax.numpy as jnp
from jax import lax
from jax.experimental import pallas as pl
from jax.experimental.pallas import tpu as pltpu
from jax.sharding import PartitionSpec as P

MESH = pl.DeviceIdType.MESH
F32 = jnp.float32
BF16 = jnp.bfloat16


def backward_rows(rows_in, grads_in, gate_mat, up_mat, down_mat):
    pre_gate = jnp.dot(rows_in, gate_mat, preferred_element_type=jnp.float32)
    pre_up = jnp.dot(rows_in, up_mat, preferred_element_type=jnp.float32)
    sigmoid_gate = jax.nn.sigmoid(pre_gate)
    activation = (pre_gate * sigmoid_gate * pre_up).astype(jnp.bfloat16)
    grad_act = jnp.dot(grads_in, down_mat, preferred_element_type=jnp.float32)
    grad_up = (grad_act * pre_gate * sigmoid_gate).astype(jnp.bfloat16)
    grad_gate = (grad_act * pre_up * sigmoid_gate * (1.0 + pre_gate * (1.0 - sigmoid_gate))).astype(
        jnp.bfloat16
    )
    grad_rows = jnp.einsum("rf,df->rd", grad_gate, gate_mat, preferred_element_type=jnp.float32)
    grad_rows = grad_rows + jnp.einsum(
        "rf,df->rd", grad_up, up_mat, preferred_element_type=jnp.float32
    )
    return (grad_rows.astype(jnp.bfloat16), grad_gate, grad_up, activation)


def on_device_routed(tokens, grad_out, expert_ids, gate_numer, w_gate, w_up, w_down):
    peers = lax.axis_size("expert")
    data_groups = lax.axis_size("dp")
    tok_rows = tokens.shape[0]
    model_width = tokens.shape[1]
    top_count = expert_ids.shape[1]
    hidden_width = w_gate.shape[2]
    mean_rows = tok_rows * top_count // peers
    capacity = min(tok_rows, mean_rows + tok_rows * top_count // (8 * peers))
    pair_count = tok_rows * top_count
    slot_count = peers * capacity
    numer = gate_numer.astype(jnp.float32)
    gate = numer / jnp.sum(numer, axis=1, keepdims=True)
    scaled = (gate[:, :, None] * grad_out.astype(jnp.float32)[:, None, :]).astype(jnp.bfloat16)
    scaled = scaled.reshape(pair_count, model_width)
    flat_ids = expert_ids.reshape(-1)
    one_hot = (flat_ids[:, None] == jnp.arange(peers, dtype=jnp.int32)[None, :]).astype(
        jnp.bfloat16
    )
    pair_range = jnp.arange(pair_count, dtype=jnp.int32)
    lower = (pair_range[None, :] < pair_range[:, None]).astype(jnp.bfloat16)
    earlier = jnp.dot(lower, one_hot, preferred_element_type=jnp.float32)
    slot = jnp.sum(earlier * one_hot.astype(jnp.float32), axis=1).astype(jnp.int32)
    target = flat_ids * capacity + slot
    pair_of_slot = jnp.full((slot_count,), pair_count, jnp.int32).at[target].set(pair_range)
    token_of_slot = jnp.where(pair_of_slot < pair_count, pair_of_slot // top_count, tok_rows)
    zero_row = jnp.zeros((1, model_width), jnp.bfloat16)
    padded_tokens = jnp.concatenate([tokens, zero_row], axis=0)
    padded_scaled = jnp.concatenate([scaled, zero_row], axis=0)
    send_rows = padded_tokens[token_of_slot].reshape(peers, capacity, model_width)
    send_grads = padded_scaled[pair_of_slot].reshape(peers, capacity, model_width)
    gathered = (
        lax.all_gather(w_gate, "dp", axis=1, tiled=True),
        lax.all_gather(w_up, "dp", axis=1, tiled=True),
        lax.all_gather(w_down, "dp", axis=1, tiled=True),
    )
    gate_mat = gathered[0][0]
    up_mat = gathered[1][0]
    down_mat = gathered[2][0]
    arrived_rows, arrived_grads = (
        lax.all_to_all(send_rows, "expert", split_axis=0, concat_axis=0, tiled=True),
        lax.all_to_all(send_grads, "expert", split_axis=0, concat_axis=0, tiled=True),
    )
    rows_in = arrived_rows.reshape(slot_count, model_width)
    grads_in = arrived_grads.reshape(slot_count, model_width)
    grad_rows, grad_gate, grad_up, activation = backward_rows(
        rows_in, grads_in, gate_mat, up_mat, down_mat
    )
    returned = lax.all_to_all(
        grad_rows.reshape(peers, capacity, model_width),
        "expert",
        split_axis=0,
        concat_axis=0,
        tiled=True,
    )
    picked = returned.reshape(slot_count, model_width)[target].astype(jnp.float32)
    grad_tokens = jnp.sum(picked.reshape(tok_rows, top_count, model_width), axis=1).astype(
        jnp.bfloat16
    )
    quarter = model_width // data_groups
    term_gate = jnp.einsum(
        "rd,rf->df", rows_in, grad_gate, preferred_element_type=jnp.float32
    ).astype(jnp.bfloat16)
    term_up = jnp.einsum("rd,rf->df", rows_in, grad_up, preferred_element_type=jnp.float32).astype(
        jnp.bfloat16
    )
    term_down = jnp.einsum(
        "rd,rf->df", grads_in, activation, preferred_element_type=jnp.float32
    ).astype(jnp.bfloat16)
    stacked = jnp.stack([term_gate, term_up, term_down]).reshape(
        3, data_groups, quarter, hidden_width
    )
    arrived = lax.all_to_all(stacked, "dp", split_axis=1, concat_axis=1, tiled=True)
    summed = jnp.sum(arrived.astype(jnp.float32), axis=1).astype(jnp.bfloat16)
    return (grad_tokens, summed[0][None], summed[1][None], summed[2][None])


def contract_rows(lhs, rhs):
    return lax.dot_general(lhs, rhs, (((0,), (0,)), ((), ())), preferred_element_type=F32)


def layer_kernel(
    chips, tok_ref, grad_ref, ids_ref, numer_ref, wg_ref, wu_ref, wd_ref,
    out_tok, out_gate, out_up, out_down,
    xbuf, gbuf, nbuf, cbuf, sbuf, obuf, rbuf, wgu, wdn, acc_gu, pbuf, qbuf, scaled, grads, acts,
    pre_buf, ga_buf, num_ref,
    w_send, w_recv, ring_send, ring_recv, sib_send, sib_recv,
    row_send, row_recv, sum_send, sum_recv, part_send, part_recv,
):
    half_ring = chips // 2
    group = lax.axis_index("dp")
    me = lax.axis_index("expert")
    core = lax.rem(me, 2)
    chip = lax.div(me, 2)
    lane = lax.rem(chip, 2)
    depth = lax.div(chip, 2)
    pos = jnp.where(lane == 0, depth, chips - 1 - depth)

    def device_at(ring_pos):
        far = ring_pos >= half_ring
        along = jnp.where(far, chips - 1 - ring_pos, ring_pos)
        return along * 4 + jnp.where(far, 2, 0) + core

    def ring(offset):
        return lax.rem(pos + offset + chips, chips)

    right = (group, device_at(ring(1)))
    left = (group, device_at(ring(-1)))
    sibling = (group, me + 1 - 2 * core)
    other = (1 - group, me)
    flows = (right, left)

    experts = 2 * chips
    expert_rows = lax.broadcasted_iota(jnp.int32, (experts, ids_ref.shape[1]), 0)
    by_expert = jnp.zeros(expert_rows.shape, jnp.int32)
    total = jnp.zeros(expert_rows.shape, jnp.int32)
    for k in range(ids_ref.shape[0]):
        numer = numer_ref[pl.ds(k, 1), :]
        by_expert = by_expert + jnp.where(ids_ref[pl.ds(k, 1), :] == expert_rows, numer, 0)
        total = total + numer
    num_ref[pl.ds(0, experts), :] = by_expert.astype(F32).astype(BF16)
    num_ref[pl.ds(experts, experts), :] = total.astype(F32).astype(BF16)

    barrier = pltpu.get_barrier_semaphore()
    for target in (right, left, sibling, other):
        pl.semaphore_signal(barrier, inc=1, device_id=target, device_id_type=MESH)
    pl.semaphore_wait(barrier, 4)

    started = []

    def copy(src, dst, send, recv, target):
        return pltpu.make_async_remote_copy(
            src_ref=src, dst_ref=dst, send_sem=send, recv_sem=recv,
            device_id=target, device_id_type=MESH,
        )

    def start(*args):
        op = copy(*args)
        op.start()
        started.append(op)

    share = wg_ref.shape[0]
    hidden = wg_ref.shape[1]
    block, width = tok_ref.shape
    own_at = pl.ds(pl.multiple_of(group * share, share), share)
    other_at = pl.ds(pl.multiple_of((1 - group) * share, share), share)

    def slot(f, d):
        return 0 if d == 0 else min(2 * d - 1 + f, chips - 1)

    bufs = (xbuf, gbuf, nbuf)
    own = (tok_ref, grad_ref, num_ref)

    def weight_places(rows):
        return (
            wgu.at[rows, pl.ds(0, hidden)],
            wgu.at[rows, pl.ds(hidden, hidden)],
            wdn.at[rows, :],
        )

    for a in (0, 2, 1):
        for f in range(2):
            start(own[a], bufs[a].at[slot(f, 1), core], ring_send.at[a, f, 0], ring_recv.at[a, f, 0], flows[f])
    weights = [
        copy(ref, weight_places(own_at)[k], w_send.at[k], w_recv.at[k], other)
        for k, ref in enumerate((wg_ref, wu_ref, wd_ref))
    ]
    for op in weights[:2]:
        op.start()
    for a in (0, 2, 1):
        start(own[a], bufs[a].at[0, core], sib_send.at[a, 0], sib_recv.at[a, 0], sibling)
    for buf, ref in ((xbuf, tok_ref), (gbuf, grad_ref), (nbuf, num_ref)):
        buf[0, core] = ref[...]
    wgu[own_at, pl.ds(0, hidden)] = wg_ref[...]
    wgu[own_at, pl.ds(hidden, hidden)] = wu_ref[...]
    wdn[own_at, :] = wd_ref[...]

    def part(a, s, c, step, f):
        if step == half_ring:
            n = bufs[a].shape[2] // 2
            return bufs[a].at[s, c, pl.ds(f * n, n)]
        return bufs[a].at[s, c]

    def arrive(a, step):
        for f in range(2):
            ref = part(a, slot(f, step), core, step, f)
            copy(ref, ref, ring_send.at[a, f, step - 1], ring_recv.at[a, f, step - 1], flows[f]).wait_recv()
            if step < half_ring:
                src = part(a, slot(f, step), core, step + 1, f)
                dst = part(a, slot(f, step + 1), core, step + 1, f)
                start(src, dst, ring_send.at[a, f, step], ring_recv.at[a, f, step], flows[f])
            k = 2 * step - 1 + f
            start(ref, ref, sib_send.at[a, k], sib_recv.at[a, k], sibling)

    def arrive_sibling(step, arrays=(0, 2, 1)):
        for a in arrays:
            for f in range(2 if step else 1):
                ref = part(a, slot(f, step), 1 - core, step, f)
                k = 2 * step - 1 + f if step else 0
                copy(ref, ref, sib_send.at[a, k], sib_recv.at[a, k], sibling).wait_recv()

    per_slot = 2 * block
    row_ids = lax.broadcasted_iota(jnp.int32, (2 * experts, 256), 0)
    col_ids = lax.broadcasted_iota(jnp.int32, (2 * experts, 256), 1)
    wanted = jnp.where(col_ids < 128, me, experts)
    select = jnp.where(row_ids == wanted, 1.0, 0.0).astype(BF16)

    def span(slots):
        return pl.ds(slots[0] * per_slot, len(slots) * per_slot)

    def tokens_of(slots, cols=slice(None)):
        return xbuf[slots[0] : slots[-1] + 1, :, :, cols].reshape(len(slots) * per_slot, -1)

    def scale(slots):
        for s in slots:
            for b in range(2):
                both = contract_rows(nbuf[s, b], select)
                gate = both[:, :128] / both[:, 128:]
                for k in range(width // 128):
                    cols = pl.ds(k * 128, 128)
                    scaled[pl.ds(s * per_slot + b * block, block), cols] = (
                        gate * gbuf[s, b, :, cols].astype(F32)
                    ).astype(BF16)

    def pre_part(slots, at):
        x = tokens_of(slots, at)
        return jnp.dot(x, wgu[at, :], preferred_element_type=F32)

    def ga_part(slots, at):
        return jnp.dot(scaled[span(slots), at], wdn[at, :], preferred_element_type=F32)

    def pointwise(slots, pre, grad_act):
        where = span(slots)
        pre_gate = pre[:, :hidden]
        pre_up = pre[:, hidden:]
        sig = jax.nn.sigmoid(pre_gate)
        silu = pre_gate * sig
        acts[where, :] = (silu * pre_up).astype(BF16)
        grads[where, pl.ds(hidden, hidden)] = (grad_act * silu).astype(BF16)
        grads[where, pl.ds(0, hidden)] = (
            grad_act * pre_up * sig * (1.0 + pre_gate * (1.0 - sig))
        ).astype(BF16)

    def back(slots):
        rows = lax.dot_general(
            grads[span(slots), :], wgu[...], (((1,), (1,)), ((), ())), preferred_element_type=F32
        )
        cbuf[slots[0] : slots[-1] + 1] = rows.astype(BF16).reshape(len(slots), 2, block, width)
        for s in slots:
            start(cbuf.at[s, 1 - core], sbuf.at[s], row_send.at[s], row_recv.at[s], sibling)

    def terms(slots, at, k):
        where = span(slots)
        if k == 2:
            return contract_rows(scaled[where, at], acts[where, :])
        return contract_rows(tokens_of(slots, at), grads[where, pl.ds(k * hidden, hidden)])

    def wait_weight(k):
        ref = weight_places(other_at)[k]
        copy(ref, ref, w_send.at[k], w_recv.at[k], other).wait_recv()

    half = block // 2
    got_rows = set()

    def row_sum(s, h):
        if s not in got_rows:
            got_rows.add(s)
            copy(sbuf.at[s], sbuf.at[s], row_send.at[s], row_recv.at[s], sibling).wait_recv()
        at = pl.ds(h * half, half)
        return cbuf[s, core, at].astype(F32) + sbuf[s, at].astype(F32)

    def order(f):
        listed = [(half_ring - 1, 1 - f), (half_ring, f), (half_ring - 1, f)]
        for d in range(half_ring - 2, 0, -1):
            listed += [(d, 1 - f), (d, f)]
        return listed

    def incoming(f, d, h):
        j = order(f).index((d + 1, h))
        ref = rbuf.at[f, j]
        copy(ref, ref, sum_send.at[f, j], sum_recv.at[f, j], flows[f]).wait_recv()
        return rbuf[f, j].astype(F32)

    def send_sums(j):
        for f in range(2):
            d, h = order(f)[j]
            value = row_sum(slot(1 - f, d), h)
            if (d + 1, h) in order(f):
                value = value + incoming(f, d, h)
            obuf[f, j] = value.astype(BF16)
            start(obuf.at[f, j], rbuf.at[f, j], sum_send.at[f, j], sum_recv.at[f, j], flows[f])

    slots_abc = [0, 1, 2, 3, 4]
    slots_a, slots_b, slots_c, slots_d, slots_e = [0], [1, 2], [3, 4], [5, 6], [7]
    everything = slice(None)

    def point(slots):
        pointwise(slots, pre_buf[span(slots), :], ga_buf[span(slots), :])

    arrive_sibling(0)
    scale(slots_a)
    pre_buf[span(slots_a), :] = pre_part(slots_a, own_at)
    ga_buf[span(slots_a), :] = ga_part(slots_a, own_at)
    arrive(0, 1)
    arrive(2, 1)
    arrive_sibling(1, (0, 2))
    pre_buf[span(slots_b), :] = pre_part(slots_b, own_at)
    arrive(1, 1)
    arrive_sibling(1, (1,))
    scale(slots_b)
    ga_buf[span(slots_b), :] = ga_part(slots_b, own_at)
    for op in weights[:2]:
        op.wait_send()
    weights[2].start()
    started.append(weights[2])
    arrive(0, 2)
    wait_weight(0)
    wait_weight(1)
    pre_buf[span(slots_a), :] += pre_part(slots_a, other_at)
    pre_buf[span(slots_b), :] += pre_part(slots_b, other_at)
    arrive(2, 2)
    arrive(1, 2)
    arrive_sibling(2, (0, 2))
    pre_buf[span(slots_c), :] = pre_part(slots_c, everything)
    arrive_sibling(2, (1,))
    scale(slots_c)
    wait_weight(2)
    ga_buf[span(slots_a), :] += ga_part(slots_a, other_at)
    point(slots_a)
    arrive(0, 3)
    arrive(2, 3)
    ga_buf[span(slots_b), :] += ga_part(slots_b, other_at)
    point(slots_b)
    ga_buf[span(slots_c), :] = ga_part(slots_c, everything)
    point(slots_c)
    arrive_sibling(3, (0, 2))
    pre_buf[span(slots_d), :] = pre_part(slots_d, everything)
    arrive(1, 3)
    for k in range(2):
        acc_gu[:, pl.ds(k * hidden, hidden)] = terms(slots_abc, other_at, k)
    arrive_sibling(3, (1,))
    scale(slots_d)
    ga_buf[span(slots_d), :] = ga_part(slots_d, everything)
    point(slots_d)
    arrive(0, 4)
    arrive(2, 4)
    back(slots_d)
    for k in range(2):
        acc_gu[:, pl.ds(k * hidden, hidden)] += terms(slots_d, other_at, k)
    arrive_sibling(4, (0, 2))
    pre_buf[span(slots_e), :] = pre_part(slots_e, everything)
    arrive(1, 4)
    arrive_sibling(4, (1,))
    scale(slots_e)
    ga_buf[span(slots_e), :] = ga_part(slots_e, everything)
    point(slots_e)

    def send_term(k):
        if k == 2:
            value = terms(list(range(chips)), other_at, k)
        else:
            value = acc_gu[:, pl.ds(k * hidden, hidden)] + terms(slots_e, other_at, k)
        pbuf[k] = value.astype(BF16)
        start(pbuf.at[k], qbuf.at[k], part_send.at[k], part_recv.at[k], other)

    send_term(0)
    send_sums(0)
    back(slots_e)
    send_term(1)

    outs = (out_gate, out_up, out_down)

    def own_term(k):
        outs[k][...] = terms(list(range(chips)), own_at, k).astype(BF16)

    between = {
        1: lambda: (send_term(2), back(slots_c)),
        2: lambda: back(slots_b),
        3: lambda: back(slots_a),
        4: lambda: own_term(0),
        5: lambda: own_term(1),
        6: lambda: own_term(2),
    }

    for j in range(1, len(order(0))):
        send_sums(j)
        if j in between:
            between[j]()
    for h in range(2):
        value = row_sum(0, h) + incoming(0, 0, h) + incoming(1, 0, h)
        out_tok[pl.ds(h * half, half), :] = value.astype(BF16)

    for k, out in enumerate(outs):
        copy(qbuf.at[k], qbuf.at[k], part_send.at[k], part_recv.at[k], other).wait_recv()
        out[...] = (out[...].astype(F32) + qbuf[k].astype(F32)).astype(BF16)
    for op in started:
        op.wait_send()


def write_out(*refs):
    ins, outs, held, sems = refs[:4], refs[4:8], refs[8:12], refs[12]
    reads = [pltpu.make_async_copy(ins[k], held[k], sems.at[k]) for k in range(4)]
    writes = [pltpu.make_async_copy(held[k], outs[k], sems.at[4 + k]) for k in range(4)]
    for op in reads:
        op.start()
    for k in range(4):
        reads[k].wait()
        writes[k].start()
    for op in writes:
        op.wait()


def on_device_dense(tokens, grad_out, expert_ids, gate_numer, w_gate, w_up, w_down):
    peers = lax.axis_size("expert")
    chips = peers // 2
    block, width = tokens.shape
    share, hidden = w_gate.shape[1:]
    depth = share * lax.axis_size("dp")
    messages = chips - 1
    rows = peers * block
    early = rows
    dma = pltpu.SemaphoreType.DMA
    vmem = pl.BlockSpec(memory_space=pltpu.VMEM)
    outs = pl.pallas_call(
        functools.partial(layer_kernel, chips),
        out_shape=(jax.ShapeDtypeStruct((block, width), BF16),)
        + (jax.ShapeDtypeStruct((share, hidden), BF16),) * 3,
        in_specs=[vmem] * 7,
        out_specs=(vmem,) * 4,
        scratch_shapes=[
            pltpu.VMEM((chips, 2, block, width), BF16),
            pltpu.VMEM((chips, 2, block, width), BF16),
            pltpu.VMEM((chips, 2, 2 * peers, block), BF16),
            pltpu.VMEM((chips, 2, block, width), BF16),
            pltpu.VMEM((chips, block, width), BF16),
            pltpu.VMEM((2, messages, block // 2, width), BF16),
            pltpu.VMEM((2, messages, block // 2, width), BF16),
            pltpu.VMEM((depth, 2 * hidden), BF16),
            pltpu.VMEM((depth, hidden), BF16),
            pltpu.VMEM((share, 2 * hidden), F32),
            pltpu.VMEM((3, share, hidden), BF16),
            pltpu.VMEM((3, share, hidden), BF16),
            pltpu.VMEM((rows, width), BF16),
            pltpu.VMEM((rows, 2 * hidden), BF16),
            pltpu.VMEM((rows, hidden), BF16),
            pltpu.VMEM((early, 2 * hidden), F32),
            pltpu.VMEM((early, hidden), F32),
            pltpu.VMEM((2 * peers, block), BF16),
            dma((3,)), dma((3,)),
            dma((3, 2, chips // 2)), dma((3, 2, chips // 2)),
            dma((3, chips + 1)), dma((3, chips + 1)),
            dma((chips,)), dma((chips,)),
            dma((2, messages)), dma((2, messages)),
            dma((3,)), dma((3,)),
        ],
        compiler_params=pltpu.CompilerParams(
            collective_id=0, has_side_effects=True, vmem_limit_bytes=58 * 1024 * 1024
        ),
        cost_estimate=pl.CostEstimate(
            flops=16 * peers * block * width * hidden, bytes_accessed=8 * block * width, transcendentals=0
        ),
    )(tokens, grad_out, expert_ids.T, gate_numer.T, w_gate[0], w_up[0], w_down[0])
    outs = pl.pallas_call(
        write_out,
        out_shape=tuple(jax.ShapeDtypeStruct(value.shape, value.dtype) for value in outs),
        in_specs=[pl.BlockSpec(memory_space=pltpu.HBM)] * 4,
        out_specs=(pl.BlockSpec(memory_space=pltpu.HBM),) * 4,
        scratch_shapes=[pltpu.VMEM(value.shape, value.dtype) for value in outs] + [dma((8,))],
    )(*outs)
    return (outs[0],) + tuple(value[None] for value in outs[1:])


def solution(mesh):
    return jax.shard_map(
        on_device_dense if mesh.shape["expert"] == 16 else on_device_routed,
        mesh=mesh,
        in_specs=(
            P(("dp", "expert"), None),
            P(("dp", "expert"), None),
            P(("dp", "expert"), None),
            P(("dp", "expert"), None),
            P("expert", "dp", None),
            P("expert", "dp", None),
            P("expert", "dp", None),
        ),
        out_specs=(
            P(("dp", "expert"), None),
            P("expert", "dp", None),
            P("expert", "dp", None),
            P("expert", "dp", None),
        ),
        check_vma=False,
    )
```
